256 devices in a mesh: lon: 16 (over z, x_lo), lat: 8 (over y, core), lev: 2 (over x_hi).
Axes of the slice: x: 4 (x_hi: 2, x_lo: 2; x = x_hi * 2 + x_lo), y: 4, z: 8, core: 2. Of those that a mesh axis runs over, the one named last changes fastest.
Arguments:
- state: float32 [5, 16, 128, 8192], P(None, 'lev', 'lat', 'lon'), may hold values from -6 to 6
- mask: int32 [16, 128, 8192], P('lev', 'lat', 'lon'), may hold values 0 or 1
- coriolis: float32 [128], P('lat'), may hold values from 0.05 to 0.3
- penetration: float32 [16], P('lev'), may hold values from 0.05 to 1
- flux_tiles: float32 [16384, 3, 512], P(('lon', 'lat')), may hold values from -4 to 4
- flux_owner: int32 [16384, 1], P(('lon', 'lat')), may hold values from 0 to 127; in each aligned block of 128 rows (0 to 127, 128 to 255, ...) at most 2 rows name the same one
- flux_row: int32 [16384], P(('lon', 'lat')), may hold values from 0 to 15
- fold_partner: int32 [8192], replicated, may hold values from 0 to 8191, as said below
Outputs:
- new_state: float32 [5, 16, 128, 8192], P(None, 'lev', 'lat', 'lon')
The draws below stay inside these ranges and needn't reach their ends.
Inputs may be any that keep to these rules, and one draw needn't show every extreme that they name: `flux_owner`: among the 128 tiles of one device at most 2 name the same owner, and some owner receives exactly 2 from some device. fold_partner[i] = (h - i) mod 8192 for one hinge column h.
All inputs are finite; a program needn't handle non-finite values. No bound on the sum of `mask` on one device may be relied on, other than what follows from the above.
Results may differ from the reference program's by a relative error of at most 0.0003.
Values sent between devices are 32-bit elements; how exact they have to be, the bound alone decides.
A program may use at most 192 MiB of HBM per device.

```python
import math
import jax
import jax.numpy as jnp
import numpy as np

CLON = 512
CLAT = 16
XT = 128
STEPS = 2
LEVELS = 16
NLAT = 128
NLON = 8192
CAP = 2
TILES = 16384
N_LON = 16
N_LAT = 8


def draw_fold_partner(key, part):
    hinge = jax.random.randint(key, (), 0, NLON, dtype=jnp.int32)
    return ((hinge - jnp.arange(NLON, dtype=jnp.int32)) % NLON).astype(jnp.int32)


def touch_ends(drawn, stream_key, low, largest):
    longest = drawn.shape.index(max(drawn.shape))
    spots = []
    for shift in (0, 1):
        where = [jax.random.randint(jax.random.fold_in(stream_key, axis), (), 0, length) for axis, length in enumerate(drawn.shape)]
        where[longest] = (where[longest] + shift) % drawn.shape[longest]
        spots.append(tuple(where))
    return drawn.at[spots[0]].set(low).at[spots[1]].set(largest)


def levels(key, shape, shards, least, largest):
    factor_of, own = 1.0, jax.random.fold_in(key, 6)
    for axis_at, shards_of in shards:
        heights = jnp.exp(jax.random.uniform(jax.random.fold_in(own, axis_at), (shards_of,), jnp.float32, least / len(shards), largest / len(shards)))
        factor_of = factor_of * jnp.repeat(heights, shape[axis_at] // shards_of).reshape([-1 if axis == axis_at else 1 for axis in range(len(shape))])
    return factor_of


def routed_block(stream_key, own, number, rows, count, top, reach, lean):
    ranking = jax.random.permutation(stream_key, count)
    crowded, usual = load_shares(count, rows * top, reach, lean, True), load_shares(count, rows * top, reach, lean, False)
    places = jnp.arange(count)

    def named(tallies, rotation):
        used = int((tallies > 0).sum())
        fixed = max(1, used // 4)
        shifted = fixed + (places - fixed + rotation * (used - fixed)) % max(1, count - fixed)
        return jnp.zeros((count,), jnp.int32).at[ranking[jnp.where(places < fixed, places, shifted)]].set(jnp.asarray(tallies, jnp.int32))

    tallies = jnp.where(number % 4 == 0, named(crowded, number // 4), named(usual, number - number // 4 - 1))
    mixed = jax.random.permutation(jax.random.fold_in(own, 3), count)
    giver, taker = mixed[0:count // 2 * 2:2], mixed[1:count // 2 * 2:2]
    slack = jnp.minimum(tallies[giver] - 1, reach - tallies[taker]) // 2
    slack = jnp.where((giver == ranking[0]) | (taker == ranking[0]) | (tallies[taker] == 0), 0, jnp.maximum(slack, 0))
    shifted = jax.random.randint(jax.random.fold_in(own, 4), (count // 2,), 0, 1 << 20) % (slack + 1)
    tallies = tallies.at[giver].add(-shifted).at[taker].add(shifted)
    items = jnp.searchsorted(jnp.cumsum(tallies), jnp.arange(rows * top), side="right").astype(jnp.int32)
    grid = items.reshape(top, rows).T
    grid = grid[jax.random.permutation(jax.random.fold_in(own, 1), rows)]
    rotation = jax.random.randint(jax.random.fold_in(own, 2), (rows, 1), 0, top)
    return jnp.take_along_axis(grid, (jnp.arange(top)[None, :] + rotation) % top, axis=1)


def load_shares(number_of, total, bound, slope, full):
    weights = [(1 << 20) // math.isqrt(rank ** slope) + 1 for rank in range(1, number_of + 1)]
    largest = bound if full else min(bound, max(-(-total // number_of), total * weights[0] // sum(weights)))
    least = 1 if total - largest >= number_of - 1 else 0
    given, spare = [largest] + [least] * (number_of - 1), total - largest - least * (number_of - 1)
    while spare > 0:
        candidates = [i for i in range(1, number_of) if given[i] < largest] or [i for i in range(1, number_of) if given[i] < bound]
        pool, left = sum([weights[i] for i in candidates]), spare
        for i in candidates:
            more = min(bound - given[i], max(1, left * weights[i] // pool), spare)
            given[i] = given[i] + more
            spare = spare - more
    return np.array(given)


def normal_values(stream_key, shape, spread, limit, pieces=(), kind=jnp.bfloat16):
    values = jax.random.normal(stream_key, shape, jnp.float32) * spread
    if len(pieces) > 0:
        values = levels(stream_key, shape, pieces, -0.22, 0.18) * values
    return jnp.clip(values, min=-limit, max=limit).astype(kind)


def setup_inputs(seed: int = 0) -> dict:
    key_list = jax.random.split(jax.random.key(seed), 9)
    state = normal_values(key_list[0], (5, LEVELS, NLAT, NLON), 1.0, 6.0, ((1, 2), (2, 8), (3, 16)), jnp.float32)
    mask = touch_ends((jax.random.randint(key_list[1], (LEVELS, NLAT, NLON), 0, 4) < 3).astype(jnp.int32), jax.random.fold_in(key_list[1], 1), 0, 1)
    coriolis = jnp.clip(jnp.exp(math.log(0.3) - 1.7917595 * jax.random.uniform(key_list[2], (NLAT,), jnp.float32) ** levels(key_list[2], (NLAT,), ((0, 8),), -0.2, 0.2)), 0.05, 0.3)
    penetration = jnp.clip(jnp.exp(math.log(1.0) - 2.9957323 * jax.random.uniform(key_list[3], (LEVELS,), jnp.float32) ** levels(key_list[3], (LEVELS,), ((0, 2),), -0.2, 0.2)), 0.05, 1.0)
    flux_tiles = normal_values(key_list[4], (TILES, 3, CLON), 0.5, 4.0, ((0, 128),), jnp.float32)
    flux_owner_keys = jax.random.split(jax.random.fold_in(key_list[5], 1), TILES // XT)
    flux_owner_turns = jax.random.permutation(jax.random.fold_in(key_list[5], 3), TILES // XT)
    flux_owner = jax.vmap(lambda own, number: routed_block(jax.random.fold_in(key_list[5], 2), own, number, XT, N_LON * N_LAT, 1, CAP, 2))(flux_owner_keys, flux_owner_turns).reshape((TILES, 1))
    flux_row = touch_ends(jax.random.randint(key_list[6], (TILES,), 0, CLAT), jax.random.fold_in(key_list[6], 1), 0, CLAT - 1).astype(jnp.int32)
    fold_partner = draw_fold_partner(jax.random.fold_in(key_list[8], 71), 0)
    return dict(state=state, mask=mask, coriolis=coriolis, penetration=penetration, flux_tiles=flux_tiles, flux_owner=flux_owner, flux_row=flux_row, fold_partner=fold_partner)


ALPHA = 0.2
BETA = 0.15
PRESS = 0.1
VISCOUS = 0.1
DIFFUSE = 0.1
ADVECT = 0.1


def surface_flux(flux_tiles, flux_owner, flux_row):
    owners = N_LON * N_LAT
    where_to = flux_owner[:, 0] * CLAT + flux_row
    total = jnp.zeros((owners * CLAT, 3, CLON), jnp.float32).at[where_to].add(flux_tiles)
    total = total.reshape(N_LON, N_LAT, CLAT, 3, CLON)
    return total.transpose(3, 1, 2, 0, 4).reshape(3, N_LAT * CLAT, N_LON * CLON)


def neighbours(field, sign, partner):
    east = jnp.roll(field, -1, axis=2)
    west = jnp.roll(field, 1, axis=2)
    north_row = sign * field[:, -1, :][:, partner]
    north = jnp.concatenate([field[:, 1:, :], north_row[:, None, :]], axis=1)
    south = jnp.concatenate([field[:, :1, :], field[:, :-1, :]], axis=1)
    return east, west, north, south


def pressure_of(temper, saline):
    buoyancy = ALPHA * temper - BETA * saline
    return PRESS * (jnp.cumsum(buoyancy, axis=0) - 0.5 * buoyancy)


def advance(state, wet, turning, absorb, forcing, partner):
    signs = (-1.0, -1.0, 1.0, 1.0, 1.0)
    pressure = pressure_of(state[2], state[3])
    east_p, west_p, north_p, south_p = neighbours(pressure, 1.0, partner)
    slope_x = 0.5 * (east_p - west_p)
    slope_y = 0.5 * (north_p - south_p)
    zonal, merid = state[0], state[1]
    result = []
    for field in range(5):
        value = state[field]
        east, west, north, south = neighbours(value, signs[field], partner)
        laplace = east + west + north + south - 4.0 * value
        if field == 0:
            trend = turning * merid - slope_x + VISCOUS * laplace
        elif field == 1:
            trend = -turning * zonal - slope_y + VISCOUS * laplace
        else:
            trend = DIFFUSE * laplace - ADVECT * (zonal * (0.5 * (east - west)) + merid * (0.5 * (north - south))) + absorb * forcing[field - 2][None]
        result.append(value + wet * trend)
    return jnp.stack(result)


def reference(state, mask, coriolis, penetration, flux_tiles, flux_owner, flux_row, fold_partner):
    forcing = surface_flux(flux_tiles, flux_owner, flux_row)
    wet = mask.astype(jnp.float32)
    turning = coriolis[None, :, None]
    absorb = penetration[:, None, None]
    for substep in range(STEPS):
        state = advance(state, wet, turning, absorb, forcing, fold_partner)
    return state
```

```python
import functools
import math

import jax
import jax.numpy as jnp
from jax import lax
from jax.experimental import pallas as pl
from jax.experimental.pallas import tpu as pltpu
from jax.sharding import PartitionSpec as P

ALPHA, BETA, PRESS = 0.2, 0.15, 0.1
VISCOUS, DIFFUSE, ADVECT = 0.1, 0.1, 0.1
F32, BF16, I32 = jnp.float32, jnp.bfloat16, jnp.int32
MESH = pl.DeviceIdType.MESH

ROWS, EXT = 16, 24


def split3(x):
    hi = x.astype(BF16)
    rest = x - hi.astype(F32)
    mid = rest.astype(BF16)
    low = (rest - mid.astype(F32)).astype(BF16)
    return hi, mid, low


def iota(shape, dim):
    return lax.broadcasted_iota(I32, shape, dim)


def substep(q, m, prefix, running, turning):
    width = q[0].shape[1]
    east = lambda a: pltpu.roll(a, width - 1, 1)
    west = lambda a: pltpu.roll(a, 1, 1)
    north = lambda a: pltpu.roll(a, EXT - 1, 0)
    south = lambda a: pltpu.roll(a, 1, 0)
    u, v = q[0], q[1]
    b = ALPHA * q[2] - BETA * q[3]
    running = running + b
    p = PRESS * (prefix + running - 0.5 * b)
    px = 0.5 * (east(p) - west(p))
    py = 0.5 * (north(p) - south(p))
    new = []
    for f in range(5):
        e, w, n, s = east(q[f]), west(q[f]), north(q[f]), south(q[f])
        lap = (e + w) + (n + s) - 4.0 * q[f]
        if f == 0:
            trend = turning * v - px + VISCOUS * lap
        elif f == 1:
            trend = VISCOUS * lap - turning * u - py
        else:
            trend = DIFFUSE * lap - (0.5 * ADVECT) * (u * (e - w) + v * (n - s))
        new.append(q[f] + m * trend)
    return new, running


def exchange_kernel(
    nlon, nlat, tiles, nk, W,
    state, mask, cor, pen, flux, owner_ref, row_ref, hinge, fold_lo, fold_hi,
    X, FX, PX,
    tbuf, mbuf, pk, got, meta, metas, dense, zgot, half, partner, frow, rowsgot, colsgot, foldgot,
    hsend, hgot, esend, egot, levs, levg, lev2s, lev2g, cors, mirror,
    ld, ms, mr, ss, sr, zs, zr, hs, hr, es, er, ls, lr, ps, pr, rs, rr, cs, cr, fs, fr,
):
    lon, lat, lev = lax.axis_index("lon"), lax.axis_index("lat"), lax.axis_index("lev")
    nz, NP = nlon // 2, 2 * nlat
    z, xl = lon // 2, lon % 2
    me = xl * nlat + lat
    HW = W // 2
    WX = W + 128
    N = NP * 2 * nz
    nfk = 6 * nk
    other = 1 - lev
    top, bottom = lat == nlat - 1, lat == 0

    def plane(p):
        return {"lon": z * 2 + p // nlat, "lat": p % nlat}

    def remote(src, dst, send, recv, device):
        return pltpu.make_async_remote_copy(
            src_ref=src, dst_ref=dst, send_sem=send, recv_sem=recv, device_id=device, device_id_type=MESH
        )

    def take(ref, sem):
        pltpu.make_async_copy(ref, ref, sem).wait()

    columns = pl.ds(pl.multiple_of(lev * HW, HW), HW)
    load_t = pltpu.make_async_copy(flux.at[:, :, columns], tbuf, ld.at[0])
    load_s = pltpu.make_async_copy(state, X.at[pl.ds(0, 5 * nk), pl.ds(0, ROWS), pl.ds(0, W)], ld.at[1])
    load_m = pltpu.make_async_copy(mask, mbuf, ld.at[2])
    load_t.start()
    load_s.start()
    load_m.start()

    barrier = pltpu.get_barrier_semaphore()

    def greet(device):
        pl.semaphore_signal(barrier, inc=1, device_id=device, device_id_type=MESH)

    def greet_plane(d, c):
        greet(plane((me + d) % NP))
        return c

    def greet_z(d, c):
        greet({"lon": ((z + d) % nz) * 2 + xl})
        return c

    lax.fori_loop(1, NP, greet_plane, 0)
    lax.fori_loop(1, nz, greet_z, 0)
    greet({"lev": other})
    for step in (1, nlon - 1):
        for l in (lev, other):
            greet({"lon": (lon + step) % nlon, "lev": l})

    @pl.when(jnp.logical_not(top))
    def _():
        greet({"lat": lat + 1, "lev": other})

    @pl.when(jnp.logical_not(bottom))
    def _():
        greet({"lat": lat - 1, "lev": other})

    @pl.when(top)
    def _():
        def greet_fold(d, c):
            greet({"lon": (lon + d) % nlon})
            greet({"lon": (lon + d) % nlon, "lev": other})
            return c

        lax.fori_loop(1, nlon, greet_fold, 0)

    owner, row = owner_ref[...], row_ref[...]
    eye = iota((tiles, tiles), 0) == iota((tiles, tiles), 1)
    upto = iota((tiles, tiles), 0) < iota((tiles, tiles), 1)
    wide = jnp.broadcast_to(owner, (tiles, tiles))
    col = jnp.sum(jnp.where(eye, wide, 0), axis=1, keepdims=True)
    slot = jnp.sum(jnp.where((col == wide) & upto, 1, 0), axis=0, keepdims=True)
    shift = int(math.log2(NP))
    to_p, to_z = owner & (NP - 1), owner >> shift
    target = to_p * (2 * nz) + slot * nz + to_z
    put = jnp.where(iota((N, tiles), 0) == target, 1.0, 0.0).astype(BF16)
    put3 = jnp.concatenate([put, put, put], axis=1)
    spot = jnp.where(iota((128, tiles), 0) == to_p * nz + to_z, 1.0, 0.0).astype(BF16)
    marks = jnp.where(iota((8, tiles), 0) == slot, (row + 1).astype(F32), 0.0).astype(BF16)
    meta[...] = lax.dot_general(marks, spot, (((1,), (1,)), ((), ())), preferred_element_type=F32)

    def pack(c):
        hi, mid, low = split3(tbuf[c])
        out = jnp.dot(put3, jnp.concatenate([hi, mid, low], axis=0), preferred_element_type=F32)
        pk[c] = out.reshape(NP, 2 * nz, HW)

    load_t.wait()
    pack(0)

    expected = (NP - 1) + (nz - 1) + 1 + 4
    extra = jnp.where(top, 2 * (nlon - 1), 1) + jnp.where(bottom, 0, 1)
    pl.semaphore_wait(barrier, expected + extra)

    def send_meta(d, c):
        p = (me + d) % NP
        remote(meta, metas.at[me], ms, mr, plane(p)).start()
        return c

    lax.fori_loop(1, NP, send_meta, 0)
    metas[me] = meta[...]

    def send_blocks(c):
        def one(d, carry):
            p = (me + d) % NP
            remote(pk.at[c, p], got.at[c, me], ss.at[c], sr.at[c], plane(p)).start()
            return carry

        lax.fori_loop(1, NP, one, 0)
        got[c, me] = pk[c, me]

    send_blocks(0)
    for c in (1, 2):
        pack(c)
        send_blocks(c)

    load_s.wait()
    load_m.wait()

    def wet(k, c):
        X[5 * nk + k, pl.ds(0, ROWS), pl.ds(0, W)] = mbuf[k].astype(F32)
        return c

    lax.fori_loop(0, nk, wet, 0)
    pair = iota((8, W), 0) // 2
    even = iota((8, W), 0) % 2 == 0

    def rows_out(g, c):
        low = jnp.zeros((8, W), F32)
        high = jnp.zeros((8, W), F32)
        is_mask = g >= (5 * nk) // 4
        for i in range(4):
            a = X[4 * g + i, pl.ds(0, 8), pl.ds(0, W)]
            b = X[4 * g + i, pl.ds(8, 8), pl.ds(0, W)]
            low = jnp.where(pair == i, pltpu.roll(a, 2 * i, 0), low)
            high = jnp.where(pair == i, pltpu.roll(b, (2 * i + 2) % 8, 0), high)
        hsend[0, g] = jnp.where(is_mask & jnp.logical_not(even), cor[0], low)
        hsend[1, g] = jnp.where(is_mask & even, cor[ROWS - 1], high)
        return c

    lax.fori_loop(0, nfk // 4, rows_out, 0)
    to_south = remote(hsend.at[0], hgot.at[0], hs.at[0], hr.at[0], {"lat": jnp.maximum(lat - 1, 0)})
    to_north = remote(hsend.at[1], hgot.at[1], hs.at[1], hr.at[1], {"lat": jnp.minimum(lat + 1, nlat - 1)})

    @pl.when(jnp.logical_not(bottom))
    def _():
        to_south.start()

    @pl.when(jnp.logical_not(top))
    def _():
        to_north.start()

    @pl.when(top)
    def _():
        shifted = hinge[0] % W
        for half_of in range(2):
            mirror[pl.ds(half_of * W, W), :] = jnp.where(
                iota((W, W), 0) + half_of * W == W + shifted - iota((W, W), 1), 1.0, 0.0
            ).astype(BF16)
        out = jnp.zeros((2 * nfk, W), F32)
        for lo, hi in zip(split3(fold_lo[...]), split3(fold_hi[...])):
            out += jnp.dot(lo, mirror[pl.ds(0, W), :], preferred_element_type=F32)
            out += jnp.dot(hi, mirror[pl.ds(W, W), :], preferred_element_type=F32)
        hgot[0] = out.reshape(nfk // 4, 8, W)

    @pl.when(bottom)
    def _():
        def fill(g, c):
            hgot[1, g] = pltpu.roll(hsend[0, g], 1, 0)
            return c

        lax.fori_loop(0, nfk // 4, fill, 0)

    take(metas.at[pl.ds(0, NP - 1)], mr)
    find = jnp.where(iota((128, N), 0) == me * nz + iota((128, N), 1) % nz, 1.0, 0.0).astype(BF16)
    known = jnp.dot(metas[...].reshape(NP * 8, 128).astype(BF16), find, preferred_element_type=F32)
    mine = iota((NP * 8, N), 1) // nz == (iota((NP * 8, N), 0) // 8) * 2 + iota((NP * 8, N), 0) % 8
    mine = mine & (iota((NP * 8, N), 0) % 8 < 2)
    named = jnp.sum(jnp.where(mine, known, 0.0), axis=0, keepdims=True)
    r_id = iota((nz * ROWS, N), 0)
    land = (r_id // ROWS == iota((nz * ROWS, N), 1) % nz) & ((r_id % ROWS + 1).astype(F32) == named)
    land = jnp.where(land, 1.0, 0.0).astype(BF16)
    land3 = jnp.concatenate([land, land, land], axis=1)

    def landed(c):
        take(got.at[c, pl.ds(0, NP - 1)], sr.at[c])
        hi, mid, low = split3(got[c].reshape(N, HW))
        out = jnp.dot(land3, jnp.concatenate([hi, mid, low], axis=0), preferred_element_type=F32)
        dense[c] = out.reshape(nz, ROWS, HW)

        def one(d, carry):
            t = (z + d) % nz
            remote(dense.at[c, t], zgot.at[c, z], zs.at[c], zr.at[c], {"lon": t * 2 + xl}).start()
            return carry

        lax.fori_loop(1, nz, one, 0)
        zgot[c, z] = dense[c, z]

    landed(0)

    @pl.when(jnp.logical_not(top))
    def _():
        to_south.wait_recv()

    @pl.when(jnp.logical_not(bottom))
    def _():
        to_north.wait_recv()

    upper = iota((8, W), 0) < 4

    def rows_in(g, c):
        n, s = hgot[0, g], hgot[1, g]
        for i in range(4):
            X[4 * g + i, pl.ds(ROWS, 8), pl.ds(0, W)] = jnp.where(
                upper, pltpu.roll(n, (8 - 2 * i) % 8, 0), pltpu.roll(s, (6 - 2 * i) % 8, 0)
            )
        return c

    lax.fori_loop(0, nfk // 4, rows_in, 0)
    lane = iota((EXT, 128), 1)

    def cols_out(f, c):
        w, e = c
        for k in range(nk):
            at = f * (2 * nk) + 2 * k
            a = X[f * nk + k, :, pl.ds(0, 128)]
            b = X[f * nk + k, :, pl.ds(W - 128, 128)]
            here = lane // 2 == f * nk + k
            w = jnp.where(here, pltpu.roll(a, at, 1), w)
            e = jnp.where(here, pltpu.roll(b, (at + 2) % 128, 1), e)
        return w, e

    w, e = lax.fori_loop(0, 6, cols_out, (jnp.zeros((EXT, 128), F32), jnp.zeros((EXT, 128), F32)))
    esend[0] = w
    esend[1] = e
    to_west = remote(esend.at[0], egot.at[0], es.at[0], er.at[0], {"lon": (lon + nlon - 1) % nlon})
    to_east = remote(esend.at[1], egot.at[1], es.at[1], er.at[1], {"lon": (lon + 1) % nlon})
    to_west.start()
    to_east.start()

    landed(1)

    to_west.wait_recv()
    to_east.wait_recv()
    fe, fw = egot[0], egot[1]

    def cols_in(f, c):
        for k in range(nk):
            at = f * (2 * nk) + 2 * k
            X[f * nk + k, :, pl.ds(W, 128)] = jnp.where(
                lane < 64, pltpu.roll(fe, (128 - at) % 128, 1), pltpu.roll(fw, (254 - at) % 128, 1)
            )
        return c

    lax.fori_loop(0, 6, cols_in, 0)

    to_lower = remote(levs, levg, ls, lr, {"lev": 1})
    to_lower2 = remote(lev2s, lev2g, ps, pr, {"lev": 1})

    @pl.when(lev == 0)
    def _():
        levs[...] = ALPHA * X[2 * nk] - BETA * X[3 * nk]

        def add(k, c):
            levs[...] += ALPHA * X[2 * nk + k] - BETA * X[3 * nk + k]
            return c

        lax.fori_loop(1, nk, add, 0)
        to_lower.start()
        levg[...] = jnp.zeros((EXT, WX), F32)

    row_id = iota((EXT, WX), 0)
    turning = jnp.where(row_id == ROWS, X[5 * nk, pl.ds(17, 1), :], X[5 * nk, pl.ds(22, 1), :])
    for i in range(ROWS):
        turning = jnp.where(row_id == i, cor[i], turning)
    cors[...] = turning

    landed(2)

    @pl.when(lev == 1)
    def _():
        to_lower.wait_recv()

    lev2s[...] = jnp.zeros((2, EXT, WX), F32)
    run = PX.at[0]
    run[...] = jnp.zeros((EXT, WX), F32)
    copy_row = (row_id == EXT - 1) & bottom

    def level(k, c):
        q = [X[f * nk + k] for f in range(5)]
        m = X[5 * nk + k]
        new, running = substep(q, m, levg[...], run[...], cors[...])
        run[...] = running
        new = [jnp.where(copy_row, a[0:1, :], a) for a in new]
        for f in range(5):
            X[f * nk + k] = new[f]
        lev2s[0] += ALPHA * new[2] - BETA * new[3]
        lev2s[1] += m * pen[k]
        return c

    lax.fori_loop(0, nk, level, 0)

    @pl.when(lev == 0)
    def _():
        to_lower2.start()
        lev2g[...] = jnp.zeros((2, EXT, WX), F32)

    for c in range(3):
        take(zgot.at[c, pl.ds(0, nz - 1)], zr.at[c])
        total = zgot[c, 0]
        for t in range(1, nz):
            total += zgot[c, t]
        half[c] = total
    for i, r in enumerate((0, ROWS - 1)):
        frow[i] = jnp.concatenate(
            [half[c, pl.ds(r, 1), pl.ds(q * 128, 128)] for c in range(3) for q in range(2)]
            + [jnp.zeros((2, 128), F32)],
            axis=0,
        )
    to_partner = remote(half, partner, ps2(rs, 0), ps2(rr, 0), {"lev": other})
    to_partner.start()
    south_at = jnp.maximum(lat - 1, 0)
    north_at = jnp.minimum(lat + 1, nlat - 1)
    down = [remote(frow.at[0], rowsgot.at[0, lev], rs.at[1 + i], rr.at[1 + i], {"lat": south_at, "lev": lev if i == 0 else other}) for i in range(2)]
    up = [remote(frow.at[1], rowsgot.at[1, lev], rs.at[3 + i], rr.at[3 + i], {"lat": north_at, "lev": lev if i == 0 else other}) for i in range(2)]

    @pl.when(jnp.logical_not(bottom))
    def _():
        for a in down:
            a.start()

    @pl.when(jnp.logical_not(top))
    def _():
        for a in up:
            a.start()

    edge = half.at[:, :, pl.ds(pl.multiple_of(lev * (HW - 128), 128), 128)]
    edge_to = (lon + nlon - 1 + 2 * lev) % nlon
    sides = [remote(edge, colsgot.at[lev], cs.at[i], cr.at[lev], {"lon": edge_to, "lev": lev if i == 0 else other}) for i in range(2)]
    for a in sides:
        a.start()

    @pl.when(top)
    def _():
        def one(d, c):
            for i in range(2):
                remote(
                    frow.at[1], foldgot.at[lev, lon], fs, fr.at[i],
                    {"lon": (lon + d) % nlon, "lev": lev if i == 0 else other},
                ).start()
            return c

        lax.fori_loop(1, nlon, one, 0)
        foldgot[lev, lon] = frow[1]

    FX[:, pl.ds(0, ROWS), pl.ds(pl.multiple_of(lev * HW, HW), HW)] = half[...]
    to_partner.wait_recv()
    FX[:, pl.ds(0, ROWS), pl.ds(pl.multiple_of(other * HW, HW), HW)] = partner[...]
    for i in range(2):
        pltpu.make_async_copy(colsgot.at[i], colsgot.at[i], cr.at[i]).wait()
    side = lax.broadcasted_iota(I32, (3, ROWS, 128), 2)
    FX[:, pl.ds(0, ROWS), pl.ds(W, 128)] = jnp.where(side < 64, colsgot[0], colsgot[1])

    first, last = iota((8, W), 0) == 0, iota((8, W), 0) == 7

    @pl.when(jnp.logical_not(bottom))
    def _():
        for i in range(2):
            up[i].wait_recv()

    @pl.when(jnp.logical_not(top))
    def _():
        for i in range(2):
            down[i].wait_recv()

    def joined(ref, c):
        return jnp.concatenate(
            [ref[h, pl.ds(2 * c + q, 1), pl.ds(0, 128)] for h in range(2) for q in range(2)], axis=1
        )

    @pl.when(top)
    def _():
        foldgot[other, lon] = jnp.concatenate(
            [partner[c, pl.ds(ROWS - 1, 1), pl.ds(q * 128, 128)] for c in range(3) for q in range(2)]
            + [jnp.zeros((2, 128), F32)],
            axis=0,
        )
        for i in range(2):
            take(foldgot.at[0, pl.ds(0, nlon - 1)], fr.at[i])
        b1 = (hinge[0] // W + nlon - lon) % nlon
        b0 = (b1 + nlon - 1) % nlon
        outs = [jnp.zeros((24, W), F32), jnp.zeros((24, W), F32)]
        for i, b in enumerate((b0, b1)):
            for h in range(2):
                tile = jnp.concatenate(split3(foldgot[h, b]), axis=0)
                for q in range(2):
                    at = i * W + h * HW + q * 128
                    keep = jnp.where(iota((24, 128), 0) % 2 == q, tile.astype(F32), 0.0).astype(BF16)
                    outs[q] += jnp.dot(keep, mirror[pl.ds(at, 128), :], preferred_element_type=F32)
        sums = [o[0:8] + o[8:16] + o[16:24] for o in outs]
        for c in range(3):
            rowsgot2(FX, c, sums[0][2 * c : 2 * c + 1] + sums[1][2 * c + 1 : 2 * c + 2], first, W)

    @pl.when(jnp.logical_not(top))
    def _():
        for c in range(3):
            rowsgot2(FX, c, joined(rowsgot.at[0], c), first, W)

    @pl.when(bottom)
    def _():
        for c in range(3):
            FX[c, pl.ds(ROWS, 8), pl.ds(0, W)] = jnp.where(
                last, FX[c, pl.ds(0, 1), pl.ds(0, W)], FX[c, pl.ds(ROWS, 8), pl.ds(0, W)]
            )

    @pl.when(jnp.logical_not(bottom))
    def _():
        for c in range(3):
            FX[c, pl.ds(ROWS, 8), pl.ds(0, W)] = jnp.where(
                last, joined(rowsgot.at[1], c), FX[c, pl.ds(ROWS, 8), pl.ds(0, W)]
            )

    FX[:, pl.ds(ROWS, 8), pl.ds(W, 128)] = jnp.zeros((3, 8, 128), F32)

    @pl.when(lev == 1)
    def _():
        to_lower2.wait_recv()

    PX[...] = lev2g[...]

    take(metas.at[pl.ds(0, NP - 1)], ms)
    for c in range(3):
        take(pk.at[c, pl.ds(0, NP - 1)], ss.at[c])
        take(dense.at[c, pl.ds(0, nz - 1)], zs.at[c])
    to_west.wait_send()
    to_east.wait_send()
    to_partner.wait_send()
    for a in sides:
        a.wait_send()

    @pl.when(lev == 0)
    def _():
        to_lower.wait_send()
        to_lower2.wait_send()

    @pl.when(jnp.logical_not(bottom))
    def _():
        to_south.wait_send()
        for a in down:
            a.wait_send()

    @pl.when(jnp.logical_not(top))
    def _():
        to_north.wait_send()
        for a in up:
            a.wait_send()

    @pl.when(top)
    def _():
        take(foldgot.at[:, pl.ds(0, nlon - 1)], fs)


def ps2(ref, i):
    return ref.at[i]


def rowsgot2(FX, c, line, first, W):
    FX[c, pl.ds(ROWS, 8), pl.ds(0, W)] = jnp.where(first, line, 0.0)


def finish_kernel(nk, W, X, FX, PX, cor, pen, out, run):
    k = pl.program_id(0)
    WX = W + 128
    row_id = iota((EXT, WX), 0)

    @pl.when(k == 0)
    def _():
        run[0] = jnp.zeros((EXT, WX), F32)
        extra = ALPHA * FX[0] - BETA * FX[1]
        run[1] = PX[0] + PX[1] * extra
        turning = jnp.zeros((EXT, WX), F32)
        for i in range(ROWS):
            turning = jnp.where(row_id == i, cor[i], turning)
        run[2] = turning

    m = X[5, 0]
    gain = m * pen[k]
    push = [gain * FX[c] for c in range(3)]
    q = [X[f, 0] + push[f - 2] if f > 1 else X[f, 0] for f in range(5)]
    new, running = substep(q, m, run[1], run[0], run[2])
    run[0] = running
    for f in range(5):
        result = new[f] + push[f - 2] if f > 1 else new[f]
        out[f, 0] = result[0:ROWS, 0:W]


def body(state, mask, coriolis, penetration, flux_tiles, flux_owner, flux_row, fold_partner):
    _, nk, rows, W = state.shape
    nlon, nlat = lax.axis_size("lon"), lax.axis_size("lat")
    tiles = flux_tiles.shape[0]
    nz, NP = nlon // 2, 2 * nlat
    N, HW, WX, nfk = NP * 2 * nz, W // 2, W + 128, 6 * nk
    hinge = fold_partner[0:1]

    with jax.named_scope("fold_rows"):
        signs = jnp.array([-1.0, -1.0, 1.0, 1.0, 1.0], F32)[:, None, None, None]
        pair = jnp.concatenate([state[:, :, rows - 1 :], state[:, :, rows - 2 : rows - 1]], axis=2) * signs
        wet = mask[:, rows - 1 :].astype(F32)
        wet = jnp.concatenate([wet, jnp.full_like(wet, coriolis[rows - 1])], axis=1)
        pair = jnp.concatenate([pair, wet[None]], axis=0).reshape(2 * nfk, W)

        def turned(block, value):
            at = lambda i: i * nlat + nlat - 1
            high = [(at(i), at((block - i) % nlon)) for i in range(nlon)]
            low = [(at(i), at((block - 1 - i) % nlon)) for i in range(nlon)]
            return lax.ppermute(value, ("lon", "lat"), low), lax.ppermute(value, ("lon", "lat"), high)

        fold_lo, fold_hi = lax.switch(hinge[0] // W, [functools.partial(turned, b) for b in range(nlon)], pair)

    vmem, smem, hbm = (pl.BlockSpec(memory_space=s) for s in (pltpu.VMEM, pltpu.SMEM, pl.ANY))
    V = lambda *s: pltpu.VMEM(s, F32)
    D = lambda *s: pltpu.SemaphoreType.DMA(s)
    X, FX, PX = pl.pallas_call(
        functools.partial(exchange_kernel, nlon, nlat, tiles, nk, W),
        out_shape=(
            jax.ShapeDtypeStruct((nfk, EXT, WX), F32),
            jax.ShapeDtypeStruct((3, EXT, WX), F32),
            jax.ShapeDtypeStruct((2, EXT, WX), F32),
        ),
        in_specs=[hbm, hbm, smem, smem, hbm, vmem, vmem, smem, vmem, vmem],
        out_specs=(vmem, vmem, vmem),
        scratch_shapes=[
            V(3, tiles, HW), pltpu.VMEM((nk, ROWS, W), I32),
            V(3, NP, 2 * nz, HW), V(3, NP, 2 * nz, HW), V(8, 128), V(NP, 8, 128),
            V(3, nz, ROWS, HW), V(3, nz, ROWS, HW), V(3, ROWS, HW), V(3, ROWS, HW),
            V(2, 8, 128), V(2, 2, 8, 128), V(2, 3, ROWS, 128), V(2, nlon, 8, 128),
            V(2, nfk // 4, 8, W), V(2, nfk // 4, 8, W), V(2, EXT, 128), V(2, EXT, 128),
            V(EXT, WX), V(EXT, WX), V(2, EXT, WX), V(2, EXT, WX), V(EXT, WX), pltpu.VMEM((2 * W, W), BF16),
            D(3), pltpu.SemaphoreType.DMA, pltpu.SemaphoreType.DMA, D(3), D(3), D(3), D(3), D(2), D(2), D(2), D(2),
            pltpu.SemaphoreType.DMA, pltpu.SemaphoreType.DMA, pltpu.SemaphoreType.DMA, pltpu.SemaphoreType.DMA,
            D(5), D(5), D(2), D(2), pltpu.SemaphoreType.DMA, D(2),
        ],
        compiler_params=pltpu.CompilerParams(
            collective_id=0, has_side_effects=True, vmem_limit_bytes=40 * 1024 * 1024
        ),
        name="exchange",
    )(
        state.reshape(5 * nk, rows, W), mask, coriolis, penetration, flux_tiles.transpose(1, 0, 2),
        flux_owner.reshape(1, tiles), flux_row.reshape(1, tiles), hinge, fold_lo, fold_hi,
    )

    return pl.pallas_call(
        functools.partial(finish_kernel, nk, W),
        grid=(nk,),
        out_shape=jax.ShapeDtypeStruct(state.shape, F32),
        in_specs=[
            pl.BlockSpec((6, 1, EXT, WX), lambda k: (0, k, 0, 0)),
            pl.BlockSpec((3, EXT, WX), lambda k: (0, 0, 0)),
            pl.BlockSpec((2, EXT, WX), lambda k: (0, 0, 0)),
            smem,
            smem,
        ],
        out_specs=pl.BlockSpec((5, 1, rows, W), lambda k: (0, k, 0, 0)),
        scratch_shapes=[V(3, EXT, WX)],
        compiler_params=pltpu.CompilerParams(vmem_limit_bytes=32 * 1024 * 1024),
        name="finish",
    )(X.reshape(6, nk, EXT, WX), FX, PX, coriolis, penetration)


def solution(mesh):
    return jax.shard_map(
        body,
        mesh=mesh,
        in_specs=(
            P(None, "lev", "lat", "lon"),
            P("lev", "lat", "lon"),
            P("lat"),
            P("lev"),
            P(("lon", "lat"), None, None),
            P(("lon", "lat"), None),
            P(("lon", "lat")),
            P(),
        ),
        out_specs=P(None, "lev", "lat", "lon"),
        check_vma=False,
    )
```

```python
import functools
import math

import jax
import jax.numpy as jnp
from jax import lax
from jax.experimental import pallas as pl
from jax.experimental.pallas import tpu as pltpu
from jax.sharding import PartitionSpec as P

ALPHA, BETA, PRESS = 0.2, 0.15, 0.1
VISCOUS, DIFFUSE, ADVECT = 0.1, 0.1, 0.1
F32, BF16, I32 = jnp.float32, jnp.bfloat16, jnp.int32
MESH = pl.DeviceIdType.MESH

ROWS, EXT = 16, 24


def split3(x):
    hi = x.astype(BF16)
    rest = x - hi.astype(F32)
    mid = rest.astype(BF16)
    low = (rest - mid.astype(F32)).astype(BF16)
    return hi, mid, low


def iota(shape, dim):
    return lax.broadcasted_iota(I32, shape, dim)


def substep(q, m, prefix, running, turning):
    width = q[0].shape[1]
    east = lambda a: pltpu.roll(a, width - 1, 1)
    west = lambda a: pltpu.roll(a, 1, 1)
    north = lambda a: pltpu.roll(a, EXT - 1, 0)
    south = lambda a: pltpu.roll(a, 1, 0)
    u, v = q[0], q[1]
    b = ALPHA * q[2] - BETA * q[3]
    running = running + b
    p = PRESS * (prefix + running - 0.5 * b)
    px = 0.5 * (east(p) - west(p))
    py = 0.5 * (north(p) - south(p))
    new = []
    for f in range(5):
        e, w, n, s = east(q[f]), west(q[f]), north(q[f]), south(q[f])
        lap = (e + w) + (n + s) - 4.0 * q[f]
        if f == 0:
            trend = turning * v - px + VISCOUS * lap
        elif f == 1:
            trend = VISCOUS * lap - turning * u - py
        else:
            trend = DIFFUSE * lap - (0.5 * ADVECT) * (u * (e - w) + v * (n - s))
        new.append(q[f] + m * trend)
    return new, running


def exchange_kernel(
    nlon, nlat, tiles, nk, W,
    state, mask, cor_hbm, pen_hbm, flux, owner_hbm, row_hbm, columns_ref,
    X, FX, PX,
    tbuf, mbuf, pk, got, meta, metas, dense, east_out, east_in, west_out, west_in, half, partner, frow, rowsgot, colsgot, foldgot,
    hsend, hgot, fold, folda, foldm, foldb, fold_rows, hinge, cor, pen, owner_ref, row_ref, esend, egot, levs, levg, lev2s, lev2g, cors, mirror,
    ld, ms, mr, ss, sr, zes, zer, zws, zwr, hs, hr, es, er, ls, lr, ps, pr, rs, rr, cs, cr, fs, fr, gas, gar, gbs, gbr,
):
    lon, lat, lev = lax.axis_index("lon"), lax.axis_index("lat"), lax.axis_index("lev")
    nz, NP = nlon // 2, 2 * nlat
    z, xl = lon // 2, lon % 2
    me = xl * nlat + lat
    HW = W // 2
    WX = W + 128
    N = NP * 2 * nz
    nfk = 6 * nk
    other = 1 - lev
    top, bottom = lat == nlat - 1, lat == 0

    def plane(p):
        return {"lon": z * 2 + p // nlat, "lat": p % nlat}

    def remote(src, dst, send, recv, device):
        return pltpu.make_async_remote_copy(
            src_ref=src, dst_ref=dst, send_sem=send, recv_sem=recv, device_id=device, device_id_type=MESH
        )

    def take(ref, sem):
        pltpu.make_async_copy(ref, ref, sem).wait()

    columns = pl.ds(pl.multiple_of(lev * HW, HW), HW)
    load_t = pltpu.make_async_copy(flux.at[:, :, columns], tbuf, ld.at[0])
    load_s = pltpu.make_async_copy(state, X.at[pl.ds(0, 5 * nk), pl.ds(0, ROWS), pl.ds(0, W)], ld.at[1])
    load_m = pltpu.make_async_copy(mask, mbuf, ld.at[2])
    load_t.start()
    load_s.start()
    load_m.start()
    smalls = [
        pltpu.make_async_copy(a, b, ld.at[4 + i])
        for i, (a, b) in enumerate(((owner_hbm, owner_ref), (row_hbm, row_ref), (cor_hbm, cor), (pen_hbm, pen)))
    ]
    for a in smalls:
        a.start()
    load_h = pltpu.make_async_copy(columns_ref.at[pl.ds(0, 1024)], hinge, ld.at[3])
    load_h.start()

    barrier = pltpu.get_barrier_semaphore()

    def greet(device):
        pl.semaphore_signal(barrier, inc=1, device_id=device, device_id_type=MESH)

    def greet_plane(d, c):
        greet(plane((me + d) % NP))
        return c

    lax.fori_loop(1, NP, greet_plane, 0)
    up_z, down_z = {"lon": ((z + 1) % nz) * 2 + xl}, {"lon": ((z + nz - 1) % nz) * 2 + xl}
    greet(up_z)
    greet(down_z)
    greet({"lev": other})
    for step in (1, nlon - 1):
        for l in (lev, other):
            greet({"lon": (lon + step) % nlon, "lev": l})

    @pl.when(jnp.logical_not(top))
    def _():
        greet({"lat": lat + 1, "lev": other})

    @pl.when(jnp.logical_not(bottom))
    def _():
        greet({"lat": lat - 1, "lev": other})

    @pl.when(top)
    def _():
        def greet_fold(d, c):
            greet({"lon": (lon + d) % nlon})
            greet({"lon": (lon + d) % nlon, "lev": other})
            return c

        lax.fori_loop(1, nlon, greet_fold, 0)

    for a in smalls:
        a.wait()
    owner, row = owner_ref[...], row_ref[...]
    eye = iota((tiles, tiles), 0) == iota((tiles, tiles), 1)
    upto = iota((tiles, tiles), 0) < iota((tiles, tiles), 1)
    wide = jnp.broadcast_to(owner, (tiles, tiles))
    col = jnp.sum(jnp.where(eye, wide, 0), axis=1, keepdims=True)
    slot = jnp.sum(jnp.where((col == wide) & upto, 1, 0), axis=0, keepdims=True)
    shift = int(math.log2(NP))
    to_p, to_z = owner & (NP - 1), owner >> shift
    target = to_p * (2 * nz) + slot * nz + to_z
    put = jnp.where(iota((N, tiles), 0) == target, 1.0, 0.0).astype(BF16)
    put3 = jnp.concatenate([put, put, put], axis=1)
    spot = jnp.where(iota((128, tiles), 0) == to_p * nz + to_z, 1.0, 0.0).astype(BF16)
    marks = jnp.where(iota((8, tiles), 0) == slot, (row + 1).astype(F32), 0.0).astype(BF16)
    meta[...] = lax.dot_general(marks, spot, (((1,), (1,)), ((), ())), preferred_element_type=F32)

    def pack(c):
        hi, mid, low = split3(tbuf[c])
        out = jnp.dot(put3, jnp.concatenate([hi, mid, low], axis=0), preferred_element_type=F32)
        pk[c] = out.reshape(NP, 2 * nz, HW)

    load_t.wait()
    pack(0)

    load_s.wait()
    load_m.wait()

    def wet(k, c):
        X[5 * nk + k, pl.ds(0, ROWS), pl.ds(0, W)] = mbuf[k].astype(F32)
        return c

    lax.fori_loop(0, nk, wet, 0)
    pair = iota((8, W), 0) // 2
    even = iota((8, W), 0) % 2 == 0

    def rows_out(g, c):
        low = jnp.zeros((8, W), F32)
        high = jnp.zeros((8, W), F32)
        is_mask = g >= (5 * nk) // 4
        for i in range(4):
            a = X[4 * g + i, pl.ds(0, 8), pl.ds(0, W)]
            b = X[4 * g + i, pl.ds(8, 8), pl.ds(0, W)]
            low = jnp.where(pair == i, pltpu.roll(a, 2 * i, 0), low)
            high = jnp.where(pair == i, pltpu.roll(b, (2 * i + 2) % 8, 0), high)
        hsend[0, g] = jnp.where(is_mask & jnp.logical_not(even), cor[0], low)
        hsend[1, g] = jnp.where(is_mask & even, cor[ROWS - 1], high)
        sign = jnp.where(g < (2 * nk) // 4, -1.0, 1.0)
        turned = sign * jnp.where(even, pltpu.roll(high, 7, 0), pltpu.roll(high, 1, 0))
        fold[g] = jnp.where(is_mask & jnp.logical_not(even), cor[ROWS - 1], turned)
        return c

    lax.fori_loop(0, nfk // 4, rows_out, 0)
    expected = (NP - 1) + 2 + 1 + 4
    extra = jnp.where(top, 2 * (nlon - 1), 1) + jnp.where(bottom, 0, 1)
    pl.semaphore_wait(barrier, expected + extra)

    spread = (-2, -1, 1, 2)
    there = [(4 * a + nlon - lon) % nlon for a in range(4)]
    first_hop = [remote(fold, folda.at[a], gas.at[a], gar.at[a], {"lon": there[a]}) for a in range(4)]
    second_hop = [
        remote(foldm, foldb.at[b + 2], gbs.at[i], gbr.at[i], {"lon": (lon + b + nlon) % nlon})
        for i, b in enumerate(spread)
    ]

    edge_of = pl.ds(0, 128)
    third_hop = remote(
        foldm.at[:, :, edge_of], foldb.at[5, :, :, edge_of], gbs.at[4], gbr.at[4], {"lon": (lon + 3) % nlon}
    )

    @pl.when(top)
    def _():
        for a in range(4):

            @pl.when(there[a] != lon)
            def _():
                first_hop[a].start()

            @pl.when(there[a] == lon)
            def _():
                folda[a] = fold[...]

    to_south = remote(hsend.at[0], hgot.at[0], hs.at[0], hr.at[0], {"lat": jnp.maximum(lat - 1, 0)})
    to_north = remote(hsend.at[1], hgot.at[1], hs.at[1], hr.at[1], {"lat": jnp.minimum(lat + 1, nlat - 1)})

    @pl.when(jnp.logical_not(bottom))
    def _():
        to_south.start()

    @pl.when(jnp.logical_not(top))
    def _():
        to_north.start()


    def send_meta(d, c):
        p = (me + d) % NP
        remote(meta, metas.at[me], ms, mr, plane(p)).start()
        return c

    lax.fori_loop(1, NP, send_meta, 0)
    metas[me] = meta[...]

    def send_blocks(c):
        def one(d, carry):
            p = (me + d) % NP
            remote(pk.at[c, p], got.at[c, me], ss.at[c], sr.at[c], plane(p)).start()
            return carry

        lax.fori_loop(1, NP, one, 0)
        got[c, me] = pk[c, me]

    send_blocks(0)
    for c in (1, 2):
        pack(c)
        send_blocks(c)

    load_h.wait()
    block, shifted = hinge[0] // W, hinge[0] % W
    digit = (block + 1) // 4

    @pl.when(top)
    def _():
        at = iota((W, WX), 1)
        at = jnp.where(at < W + 64, at, at - WX)
        for i in range(3):
            wide = W if i < 2 else 128
            mirror[pl.ds(i * W, wide), :] = jnp.where(
                iota((wide, WX), 0) + i * W == W + shifted - at[0:wide], 1.0, 0.0
            ).astype(BF16)

        def clear(g, c):
            hgot[0, g] = jnp.zeros((8, W), F32)
            return c

        lax.fori_loop(0, nfk // 4, clear, 0)

    @pl.when(bottom)
    def _():
        def fill(g, c):
            hgot[1, g] = pltpu.roll(hsend[0, g], 1, 0)
            return c

        lax.fori_loop(0, nfk // 4, fill, 0)

    take(metas.at[pl.ds(0, NP - 1)], mr)
    find = jnp.where(iota((128, N), 0) == me * nz + iota((128, N), 1) % nz, 1.0, 0.0).astype(BF16)
    known = jnp.dot(metas[...].reshape(NP * 8, 128).astype(BF16), find, preferred_element_type=F32)
    mine = iota((NP * 8, N), 1) // nz == (iota((NP * 8, N), 0) // 8) * 2 + iota((NP * 8, N), 0) % 8
    mine = mine & (iota((NP * 8, N), 0) % 8 < 2)
    named = jnp.sum(jnp.where(mine, known, 0.0), axis=0, keepdims=True)
    r_id = iota((nz * ROWS, N), 0)
    land = (r_id // ROWS == iota((nz * ROWS, N), 1) % nz) & ((r_id % ROWS + 1).astype(F32) == named)
    land = jnp.where(land, 1.0, 0.0).astype(BF16)
    land3 = jnp.concatenate([land, land, land], axis=1)

    ahead = nz // 2
    behind = nz - 1 - ahead

    def hop(c, s, up):
        out, into, send, recv, to = (
            (east_out, east_in, zes, zer, up_z) if up else (west_out, west_in, zws, zwr, down_z)
        )
        return remote(out.at[c, s], into.at[c, s], send.at[c, s], recv.at[c, s], to)

    def ring(c, s):
        for up, steps in ((True, ahead), (False, behind)):
            if s >= steps:
                continue
            out, into = (east_out, east_in) if up else (west_out, west_in)
            block = dense[c, (z + (steps - s if up else nz - steps + s)) % nz]
            if s > 0:
                hop(c, s - 1, up).wait_recv()
                block += into[c, s - 1]
            out[c, s] = block
            hop(c, s, up).start()

    def landed(c):
        take(got.at[c, pl.ds(0, NP - 1)], sr.at[c])
        hi, mid, low = split3(got[c].reshape(N, HW))
        out = jnp.dot(land3, jnp.concatenate([hi, mid, low], axis=0), preferred_element_type=F32)
        dense[c] = out.reshape(nz, ROWS, HW)

        ring(c, 0)

    @pl.when(jnp.logical_not(top))
    def _():
        to_south.wait_recv()

    @pl.when(jnp.logical_not(bottom))
    def _():
        to_north.wait_recv()

    upper = iota((8, W), 0) < 4

    def rows_in(g, c):
        n, s = hgot[0, g], hgot[1, g]
        for i in range(4):
            X[4 * g + i, pl.ds(ROWS, 8), pl.ds(0, W)] = jnp.where(
                upper, pltpu.roll(n, (8 - 2 * i) % 8, 0), pltpu.roll(s, (6 - 2 * i) % 8, 0)
            )
        return c

    lax.fori_loop(0, nfk // 4, rows_in, 0)
    lane = iota((EXT, 128), 1)

    def cols_out(f, c):
        w, e = c
        for k in range(nk):
            at = f * (2 * nk) + 2 * k
            a = X[f * nk + k, :, pl.ds(0, 128)]
            b = X[f * nk + k, :, pl.ds(W - 128, 128)]
            here = lane // 2 == f * nk + k
            w = jnp.where(here, pltpu.roll(a, at, 1), w)
            e = jnp.where(here, pltpu.roll(b, (at + 2) % 128, 1), e)
        return w, e

    w, e = lax.fori_loop(0, 6, cols_out, (jnp.zeros((EXT, 128), F32), jnp.zeros((EXT, 128), F32)))
    esend[0] = w
    esend[1] = e
    to_west = remote(esend.at[0], egot.at[0], es.at[0], er.at[0], {"lon": (lon + nlon - 1) % nlon})
    to_east = remote(esend.at[1], egot.at[1], es.at[1], er.at[1], {"lon": (lon + 1) % nlon})
    to_west.start()
    to_east.start()

    for c in range(3):
        landed(c)
    to_west.wait_recv()
    to_east.wait_recv()
    fe, fw = egot[0], egot[1]

    def cols_in(f, c):
        for k in range(nk):
            at = f * (2 * nk) + 2 * k
            X[f * nk + k, :, pl.ds(W, 128)] = jnp.where(
                lane < 64, pltpu.roll(fe, (128 - at) % 128, 1), pltpu.roll(fw, (254 - at) % 128, 1)
            )
        return c

    lax.fori_loop(0, 6, cols_in, 0)

    for c in range(3):
        ring(c, 1)

    @pl.when(top)
    def _():
        for a in range(4):

            @pl.when(there[a] != lon)
            def _():
                first_hop[a].wait_recv()

        def pick(g, c):
            foldm[g] = folda[digit % 4, g]
            foldb[2, g] = folda[digit % 4, g]
            return c

        lax.fori_loop(0, nfk // 4, pick, 0)
        for a in second_hop:
            a.start()
        third_hop.start()

    for s in range(2, ahead):
        for c in range(3):
            ring(c, s)

    for c in range(3):
        hop(c, ahead - 1, True).wait_recv()
        total = dense[c, z] + east_in[c, ahead - 1]
        if behind:
            hop(c, behind - 1, False).wait_recv()
            total += west_in[c, behind - 1]
        half[c] = total
    for i, r in enumerate((0, ROWS - 1)):
        frow[i] = jnp.concatenate(
            [half[c, pl.ds(r, 1), pl.ds(q * 128, 128)] for c in range(3) for q in range(2)]
            + [jnp.zeros((2, 128), F32)],
            axis=0,
        )
    to_partner = remote(half, partner, ps2(rs, 0), ps2(rr, 0), {"lev": other})
    to_partner.start()
    south_at = jnp.maximum(lat - 1, 0)
    north_at = jnp.minimum(lat + 1, nlat - 1)
    down = [remote(frow.at[0], rowsgot.at[0, lev], rs.at[1 + i], rr.at[1 + i], {"lat": south_at, "lev": lev if i == 0 else other}) for i in range(2)]
    up = [remote(frow.at[1], rowsgot.at[1, lev], rs.at[3 + i], rr.at[3 + i], {"lat": north_at, "lev": lev if i == 0 else other}) for i in range(2)]

    @pl.when(jnp.logical_not(bottom))
    def _():
        for a in down:
            a.start()

    @pl.when(jnp.logical_not(top))
    def _():
        for a in up:
            a.start()

    edge = half.at[:, :, pl.ds(pl.multiple_of(lev * (HW - 128), 128), 128)]
    edge_to = (lon + nlon - 1 + 2 * lev) % nlon
    sides = [remote(edge, colsgot.at[lev], cs.at[i], cr.at[lev], {"lon": edge_to, "lev": lev if i == 0 else other}) for i in range(2)]
    for a in sides:
        a.start()

    @pl.when(top)
    def _():
        def one(d, c):
            for i in range(2):
                remote(
                    frow.at[1], foldgot.at[lev, lon], fs, fr.at[i],
                    {"lon": (lon + d) % nlon, "lev": lev if i == 0 else other},
                ).start()
            return c

        lax.fori_loop(1, nlon, one, 0)
        foldgot[lev, lon] = frow[1]

    @pl.when(top)
    def _():
        for a in second_hop:
            a.wait_recv()
        third_hop.wait_recv()
        near = block - 4 * digit + 1
        out = jnp.zeros((2 * nfk, WX), F32)
        for i in range(3):
            wide = W if i < 2 else 128
            for part in split3(foldb[near + i, :, :, pl.ds(0, wide)].reshape(2 * nfk, wide)):
                out += jnp.dot(part, mirror[pl.ds(i * W, wide), :], preferred_element_type=F32)
        fold_rows[...] = out.reshape(nfk // 4, 8, WX)
        two = iota((8, WX), 0) < 2

        def insert(g, c):
            n = fold_rows[g]
            for i in range(4):
                X[4 * g + i, pl.ds(ROWS, 8), :] = jnp.where(
                    two, pltpu.roll(n, (8 - 2 * i) % 8, 0), X[4 * g + i, pl.ds(ROWS, 8), :]
                )
            return c

        lax.fori_loop(0, nfk // 4, insert, 0)

    to_lower = remote(levs, levg, ls, lr, {"lev": 1})
    to_lower2 = remote(lev2s, lev2g, ps, pr, {"lev": 1})

    @pl.when(lev == 0)
    def _():
        levs[...] = ALPHA * X[2 * nk] - BETA * X[3 * nk]

        def add(k, c):
            levs[...] += ALPHA * X[2 * nk + k] - BETA * X[3 * nk + k]
            return c

        lax.fori_loop(1, nk, add, 0)
        to_lower.start()
        levg[...] = jnp.zeros((EXT, WX), F32)

    row_id = iota((EXT, WX), 0)
    turning = jnp.where(row_id == ROWS, X[5 * nk, pl.ds(17, 1), :], X[5 * nk, pl.ds(22, 1), :])
    for i in range(ROWS):
        turning = jnp.where(row_id == i, cor[i], turning)
    cors[...] = turning

    @pl.when(lev == 1)
    def _():
        to_lower.wait_recv()

    lev2s[...] = jnp.zeros((2, EXT, WX), F32)
    run = PX.at[0]
    run[...] = jnp.zeros((EXT, WX), F32)
    copy_row = (row_id == EXT - 1) & bottom

    def level(k, c):
        q = [X[f * nk + k] for f in range(5)]
        m = X[5 * nk + k]
        new, running = substep(q, m, levg[...], run[...], cors[...])
        run[...] = running
        new = [jnp.where(copy_row, a[0:1, :], a) for a in new]
        for f in range(5):
            X[f * nk + k] = new[f]
        lev2s[0] += ALPHA * new[2] - BETA * new[3]
        lev2s[1] += m * pen[k]
        return c

    lax.fori_loop(0, nk, level, 0)

    @pl.when(lev == 0)
    def _():
        to_lower2.start()
        lev2g[...] = jnp.zeros((2, EXT, WX), F32)

    FX[:, pl.ds(0, ROWS), pl.ds(pl.multiple_of(lev * HW, HW), HW)] = half[...]
    to_partner.wait_recv()
    FX[:, pl.ds(0, ROWS), pl.ds(pl.multiple_of(other * HW, HW), HW)] = partner[...]
    for i in range(2):
        pltpu.make_async_copy(colsgot.at[i], colsgot.at[i], cr.at[i]).wait()
    side = lax.broadcasted_iota(I32, (3, ROWS, 128), 2)
    FX[:, pl.ds(0, ROWS), pl.ds(W, 128)] = jnp.where(side < 64, colsgot[0], colsgot[1])

    first, last = iota((8, W), 0) == 0, iota((8, W), 0) == 7

    @pl.when(jnp.logical_not(bottom))
    def _():
        for i in range(2):
            up[i].wait_recv()

    @pl.when(jnp.logical_not(top))
    def _():
        for i in range(2):
            down[i].wait_recv()

    def joined(ref, c):
        return jnp.concatenate(
            [ref[h, pl.ds(2 * c + q, 1), pl.ds(0, 128)] for h in range(2) for q in range(2)], axis=1
        )

    @pl.when(top)
    def _():
        foldgot[other, lon] = jnp.concatenate(
            [partner[c, pl.ds(ROWS - 1, 1), pl.ds(q * 128, 128)] for c in range(3) for q in range(2)]
            + [jnp.zeros((2, 128), F32)],
            axis=0,
        )
        for i in range(2):
            take(foldgot.at[0, pl.ds(0, nlon - 1)], fr.at[i])
        b1 = (block + nlon - lon) % nlon
        b0 = (b1 + nlon - 1) % nlon
        outs = [jnp.zeros((24, W), F32), jnp.zeros((24, W), F32)]
        for i, b in enumerate((b0, b1)):
            for h in range(2):
                tile = jnp.concatenate(split3(foldgot[h, b]), axis=0)
                for q in range(2):
                    at = i * W + h * HW + q * 128
                    keep = jnp.where(iota((24, 128), 0) % 2 == q, tile.astype(F32), 0.0).astype(BF16)
                    outs[q] += jnp.dot(keep, mirror[pl.ds(at, 128), pl.ds(0, W)], preferred_element_type=F32)
        sums = [o[0:8] + o[8:16] + o[16:24] for o in outs]
        for c in range(3):
            rowsgot2(FX, c, sums[0][2 * c : 2 * c + 1] + sums[1][2 * c + 1 : 2 * c + 2], first, W)

    @pl.when(jnp.logical_not(top))
    def _():
        for c in range(3):
            rowsgot2(FX, c, joined(rowsgot.at[0], c), first, W)

    @pl.when(bottom)
    def _():
        for c in range(3):
            FX[c, pl.ds(ROWS, 8), pl.ds(0, W)] = jnp.where(
                last, FX[c, pl.ds(0, 1), pl.ds(0, W)], FX[c, pl.ds(ROWS, 8), pl.ds(0, W)]
            )

    @pl.when(jnp.logical_not(bottom))
    def _():
        for c in range(3):
            FX[c, pl.ds(ROWS, 8), pl.ds(0, W)] = jnp.where(
                last, joined(rowsgot.at[1], c), FX[c, pl.ds(ROWS, 8), pl.ds(0, W)]
            )

    FX[:, pl.ds(ROWS, 8), pl.ds(W, 128)] = jnp.zeros((3, 8, 128), F32)

    @pl.when(lev == 1)
    def _():
        to_lower2.wait_recv()

    PX[...] = lev2g[...]

    take(metas.at[pl.ds(0, NP - 1)], ms)
    for c in range(3):
        take(pk.at[c, pl.ds(0, NP - 1)], ss.at[c])
        for s in range(ahead):
            hop(c, s, True).wait_send()
        for s in range(behind):
            hop(c, s, False).wait_send()
    to_west.wait_send()
    to_east.wait_send()
    to_partner.wait_send()
    for a in sides:
        a.wait_send()

    @pl.when(lev == 0)
    def _():
        to_lower.wait_send()
        to_lower2.wait_send()

    @pl.when(jnp.logical_not(bottom))
    def _():
        to_south.wait_send()
        for a in down:
            a.wait_send()

    @pl.when(jnp.logical_not(top))
    def _():
        to_north.wait_send()
        for a in up:
            a.wait_send()

    @pl.when(top)
    def _():
        take(foldgot.at[:, pl.ds(0, nlon - 1)], fs)
        for a in range(4):

            @pl.when(there[a] != lon)
            def _():
                first_hop[a].wait_send()

        for a in second_hop:
            a.wait_send()
        third_hop.wait_send()


def ps2(ref, i):
    return ref.at[i]


def rowsgot2(FX, c, line, first, W):
    FX[c, pl.ds(ROWS, 8), pl.ds(0, W)] = jnp.where(first, line, 0.0)


def finish_kernel(nk, W, X, FX, PX, cor, pen, out, run):
    k = pl.program_id(0)
    WX = W + 128
    row_id = iota((EXT, WX), 0)

    @pl.when(k == 0)
    def _():
        run[0] = jnp.zeros((EXT, WX), F32)
        extra = ALPHA * FX[0] - BETA * FX[1]
        run[1] = PX[0] + PX[1] * extra
        turning = jnp.zeros((EXT, WX), F32)
        for i in range(ROWS):
            turning = jnp.where(row_id == i, cor[i], turning)
        run[2] = turning

    m = X[5, 0]
    gain = m * pen[k]
    push = [gain * FX[c] for c in range(3)]
    q = [X[f, 0] + push[f - 2] if f > 1 else X[f, 0] for f in range(5)]
    new, running = substep(q, m, run[1], run[0], run[2])
    run[0] = running
    for f in range(5):
        result = new[f] + push[f - 2] if f > 1 else new[f]
        out[f, 0] = result[0:ROWS, 0:W]


def body(state, mask, coriolis, penetration, flux_tiles, flux_owner, flux_row, fold_partner):
    _, nk, rows, W = state.shape
    nlon, nlat = lax.axis_size("lon"), lax.axis_size("lat")
    tiles = flux_tiles.shape[0]
    nz, NP = nlon // 2, 2 * nlat
    N, HW, WX, nfk = NP * 2 * nz, W // 2, W + 128, 6 * nk

    up, down = nz // 2, max(1, nz - 1 - nz // 2)
    vmem, smem, hbm = (pl.BlockSpec(memory_space=s) for s in (pltpu.VMEM, pltpu.SMEM, pltpu.HBM))
    V = lambda *s: pltpu.VMEM(s, F32)
    D = lambda *s: pltpu.SemaphoreType.DMA(s)
    X, FX, PX = pl.pallas_call(
        functools.partial(exchange_kernel, nlon, nlat, tiles, nk, W),
        out_shape=(
            jax.ShapeDtypeStruct((nfk, EXT, WX), F32),
            jax.ShapeDtypeStruct((3, EXT, WX), F32),
            jax.ShapeDtypeStruct((2, EXT, WX), F32),
        ),
        in_specs=[hbm] * 8,
        out_specs=(vmem, vmem, vmem),
        scratch_shapes=[
            V(3, tiles, HW), pltpu.VMEM((nk, ROWS, W), I32),
            V(3, NP, 2 * nz, HW), V(3, NP, 2 * nz, HW), V(8, 128), V(NP, 8, 128),
            V(3, nz, ROWS, HW), V(3, up, ROWS, HW), V(3, up, ROWS, HW), V(3, down, ROWS, HW), V(3, down, ROWS, HW),
            V(3, ROWS, HW), V(3, ROWS, HW),
            V(2, 8, 128), V(2, 2, 8, 128), V(2, 3, ROWS, 128), V(2, nlon, 8, 128),
            V(2, nfk // 4, 8, W), V(2, nfk // 4, 8, W),
            V(nfk // 4, 8, W), V(4, nfk // 4, 8, W), V(nfk // 4, 8, W), V(6, nfk // 4, 8, W), V(nfk // 4, 8, WX), pltpu.SMEM((1024,), I32),
            pltpu.SMEM((ROWS,), F32), pltpu.SMEM((nk,), F32), pltpu.VMEM((1, tiles), I32), pltpu.VMEM((1, tiles), I32),
            V(2, EXT, 128), V(2, EXT, 128),
            V(EXT, WX), V(EXT, WX), V(2, EXT, WX), V(2, EXT, WX), V(EXT, WX), pltpu.VMEM((2 * W + 128, WX), BF16),
            D(8), pltpu.SemaphoreType.DMA, pltpu.SemaphoreType.DMA, D(3), D(3), D(3, up), D(3, up), D(3, down), D(3, down), D(2), D(2), D(2), D(2),
            pltpu.SemaphoreType.DMA, pltpu.SemaphoreType.DMA, pltpu.SemaphoreType.DMA, pltpu.SemaphoreType.DMA,
            D(5), D(5), D(2), D(2), pltpu.SemaphoreType.DMA, D(2), D(4), D(4), D(5), D(5),
        ],
        compiler_params=pltpu.CompilerParams(
            collective_id=0, has_side_effects=True, vmem_limit_bytes=60 * 1024 * 1024
        ),
        name="exchange",
    )(
        state.reshape(5 * nk, rows, W), mask, coriolis, penetration, flux_tiles.transpose(1, 0, 2),
        flux_owner.reshape(1, tiles), flux_row.reshape(1, tiles), fold_partner,
    )

    return pl.pallas_call(
        functools.partial(finish_kernel, nk, W),
        grid=(nk,),
        out_shape=jax.ShapeDtypeStruct(state.shape, F32),
        in_specs=[
            pl.BlockSpec((6, 1, EXT, WX), lambda k: (0, k, 0, 0)),
            pl.BlockSpec((3, EXT, WX), lambda k: (0, 0, 0)),
            pl.BlockSpec((2, EXT, WX), lambda k: (0, 0, 0)),
            smem,
            smem,
        ],
        out_specs=pl.BlockSpec((5, 1, rows, W), lambda k: (0, k, 0, 0)),
        scratch_shapes=[V(3, EXT, WX)],
        compiler_params=pltpu.CompilerParams(vmem_limit_bytes=32 * 1024 * 1024),
        name="finish",
    )(X.reshape(6, nk, EXT, WX), FX, PX, coriolis, penetration)


def solution(mesh):
    return jax.shard_map(
        body,
        mesh=mesh,
        in_specs=(
            P(None, "lev", "lat", "lon"),
            P("lev", "lat", "lon"),
            P("lat"),
            P("lev"),
            P(("lon", "lat"), None, None),
            P(("lon", "lat"), None),
            P(("lon", "lat")),
            P(),
        ),
        out_specs=P(None, "lev", "lat", "lon"),
        check_vma=False,
    )
```

```python
import functools
import math

import jax
import jax.numpy as jnp
from jax import lax
from jax.experimental import pallas as pl
from jax.experimental.pallas import tpu as pltpu
from jax.sharding import PartitionSpec as P

ALPHA, BETA, PRESS = 0.2, 0.15, 0.1
VISCOUS, DIFFUSE, ADVECT = 0.1, 0.1, 0.1
F32, BF16, I32 = jnp.float32, jnp.bfloat16, jnp.int32
MESH = pl.DeviceIdType.MESH

ROWS, EXT = 16, 24


def split3(x):
    hi = x.astype(BF16)
    rest = x - hi.astype(F32)
    mid = rest.astype(BF16)
    low = (rest - mid.astype(F32)).astype(BF16)
    return hi, mid, low


def iota(shape, dim):
    return lax.broadcasted_iota(I32, shape, dim)


def substep(q, m, prefix, running, turning):
    width = q[0].shape[1]
    east = lambda a: pltpu.roll(a, width - 1, 1)
    west = lambda a: pltpu.roll(a, 1, 1)
    north = lambda a: pltpu.roll(a, EXT - 1, 0)
    south = lambda a: pltpu.roll(a, 1, 0)
    u, v = q[0], q[1]
    b = ALPHA * q[2] - BETA * q[3]
    running = running + b
    p = PRESS * (prefix + running - 0.5 * b)
    px = 0.5 * (east(p) - west(p))
    py = 0.5 * (north(p) - south(p))
    new = []
    for f in range(5):
        e, w, n, s = east(q[f]), west(q[f]), north(q[f]), south(q[f])
        lap = (e + w) + (n + s) - 4.0 * q[f]
        if f == 0:
            trend = turning * v - px + VISCOUS * lap
        elif f == 1:
            trend = VISCOUS * lap - turning * u - py
        else:
            trend = DIFFUSE * lap - (0.5 * ADVECT) * (u * (e - w) + v * (n - s))
        new.append(q[f] + m * trend)
    return new, running


def exchange_kernel(
    nlon, nlat, tiles, nk, W,
    state, mask, cor_hbm, pen_hbm, flux, owner_hbm, row_hbm, columns_ref,
    result,
    X, FX, tail, outs, tbuf, mbuf, pk, got, meta, metas, dense, east_out, east_in, west_out, west_in, half, partner, frow, rowsgot, colsgot, foldgot,
    hsend, hgot, fold, folda, foldm, foldb, fold_rows, hinge, cor, pen, owner_ref, row_ref, esend, egot, levs, levg, lev2s, lev2g, cors, mirror,
    ld, ms, mr, ss, sr, zes, zer, zws, zwr, hs, hr, es, er, ls, lr, ps, pr, rs, rr, cs, cr, fs, fr, gas, gar, gbs, gbr, ds,
):
    lon, lat, lev = lax.axis_index("lon"), lax.axis_index("lat"), lax.axis_index("lev")
    nz, NP = nlon // 2, 2 * nlat
    z, xl = lon // 2, lon % 2
    me = xl * nlat + lat
    HW = W // 2
    WX = W + 128
    N = NP * 2 * nz
    nfk = 6 * nk
    other = 1 - lev
    top, bottom = lat == nlat - 1, lat == 0

    def plane(p):
        return {"lon": z * 2 + p // nlat, "lat": p % nlat}

    def remote(src, dst, send, recv, device):
        return pltpu.make_async_remote_copy(
            src_ref=src, dst_ref=dst, send_sem=send, recv_sem=recv, device_id=device, device_id_type=MESH
        )

    def take(ref, sem):
        pltpu.make_async_copy(ref, ref, sem).wait()

    columns = pl.ds(pl.multiple_of(lev * HW, HW), HW)
    load_t = pltpu.make_async_copy(flux.at[:, :, columns], tbuf, ld.at[0])
    load_s = pltpu.make_async_copy(state, X.at[pl.ds(0, 5 * nk), pl.ds(0, ROWS), pl.ds(0, W)], ld.at[1])
    load_m = pltpu.make_async_copy(mask, mbuf, ld.at[2])
    load_t.start()
    load_s.start()
    load_m.start()
    smalls = [
        pltpu.make_async_copy(a, b, ld.at[4 + i])
        for i, (a, b) in enumerate(((owner_hbm, owner_ref), (row_hbm, row_ref), (cor_hbm, cor), (pen_hbm, pen)))
    ]
    for a in smalls:
        a.start()
    load_h = pltpu.make_async_copy(columns_ref.at[pl.ds(0, 1024)], hinge, ld.at[3])
    load_h.start()

    barrier = pltpu.get_barrier_semaphore()

    def greet(device):
        pl.semaphore_signal(barrier, inc=1, device_id=device, device_id_type=MESH)

    def greet_plane(d, c):
        greet(plane((me + d) % NP))
        return c

    lax.fori_loop(1, NP, greet_plane, 0)
    up_z, down_z = {"lon": ((z + 1) % nz) * 2 + xl}, {"lon": ((z + nz - 1) % nz) * 2 + xl}
    greet(up_z)
    greet(down_z)
    greet({"lev": other})
    for step in (1, nlon - 1):
        for l in (lev, other):
            greet({"lon": (lon + step) % nlon, "lev": l})

    @pl.when(jnp.logical_not(top))
    def _():
        greet({"lat": lat + 1, "lev": other})

    @pl.when(jnp.logical_not(bottom))
    def _():
        greet({"lat": lat - 1, "lev": other})

    @pl.when(top)
    def _():
        def greet_fold(d, c):
            greet({"lon": (lon + d) % nlon})
            greet({"lon": (lon + d) % nlon, "lev": other})
            return c

        lax.fori_loop(1, nlon, greet_fold, 0)

    for a in smalls:
        a.wait()
    owner, row = owner_ref[...], row_ref[...]
    eye = iota((tiles, tiles), 0) == iota((tiles, tiles), 1)
    upto = iota((tiles, tiles), 0) < iota((tiles, tiles), 1)
    wide = jnp.broadcast_to(owner, (tiles, tiles))
    col = jnp.sum(jnp.where(eye, wide, 0), axis=1, keepdims=True)
    slot = jnp.sum(jnp.where((col == wide) & upto, 1, 0), axis=0, keepdims=True)
    shift = int(math.log2(NP))
    to_p, to_z = owner & (NP - 1), owner >> shift
    target = to_p * (2 * nz) + slot * nz + to_z
    put = jnp.where(iota((N, tiles), 0) == target, 1.0, 0.0).astype(BF16)
    put3 = jnp.concatenate([put, put, put], axis=1)
    spot = jnp.where(iota((128, tiles), 0) == to_p * nz + to_z, 1.0, 0.0).astype(BF16)
    marks = jnp.where(iota((8, tiles), 0) == slot, (row + 1).astype(F32), 0.0).astype(BF16)
    meta[...] = lax.dot_general(marks, spot, (((1,), (1,)), ((), ())), preferred_element_type=F32)

    def pack(c):
        hi, mid, low = split3(tbuf[c])
        out = jnp.dot(put3, jnp.concatenate([hi, mid, low], axis=0), preferred_element_type=F32)
        pk[c] = out.reshape(NP, 2 * nz, HW)

    load_t.wait()
    for c in range(3):
        pack(c)

    load_s.wait()
    load_m.wait()

    def wet(k, c):
        X[5 * nk + k, pl.ds(0, ROWS), pl.ds(0, W)] = mbuf[k].astype(F32)
        return c

    lax.fori_loop(0, nk, wet, 0)
    pair = iota((8, W), 0) // 2
    even = iota((8, W), 0) % 2 == 0

    def rows_out(g, c):
        low = jnp.zeros((8, W), F32)
        high = jnp.zeros((8, W), F32)
        is_mask = g >= (5 * nk) // 4
        for i in range(4):
            a = X[4 * g + i, pl.ds(0, 8), pl.ds(0, W)]
            b = X[4 * g + i, pl.ds(8, 8), pl.ds(0, W)]
            low = jnp.where(pair == i, pltpu.roll(a, 2 * i, 0), low)
            high = jnp.where(pair == i, pltpu.roll(b, (2 * i + 2) % 8, 0), high)
        hsend[0, g] = jnp.where(is_mask & jnp.logical_not(even), cor[0], low)
        hsend[1, g] = jnp.where(is_mask & even, cor[ROWS - 1], high)
        sign = jnp.where(g < (2 * nk) // 4, -1.0, 1.0)
        turned = sign * jnp.where(even, pltpu.roll(high, 7, 0), pltpu.roll(high, 1, 0))
        fold[g] = jnp.where(is_mask & jnp.logical_not(even), cor[ROWS - 1], turned)
        return c

    lax.fori_loop(0, nfk // 4, rows_out, 0)
    expected = (NP - 1) + 2 + 1 + 4
    extra = jnp.where(top, 2 * (nlon - 1), 1) + jnp.where(bottom, 0, 1)
    pl.semaphore_wait(barrier, expected + extra)

    spread = (-2, -1, 1, 2)
    there = [(4 * a + nlon - lon) % nlon for a in range(4)]
    first_hop = [remote(fold, folda.at[a], gas.at[a], gar.at[a], {"lon": there[a]}) for a in range(4)]
    second_hop = [
        remote(foldm, foldb.at[b + 2], gbs.at[i], gbr.at[i], {"lon": (lon + b + nlon) % nlon})
        for i, b in enumerate(spread)
    ]

    edge_of = pl.ds(0, 128)
    third_hop = remote(
        foldm.at[:, :, edge_of], foldb.at[5, :, :, edge_of], gbs.at[4], gbr.at[4], {"lon": (lon + 3) % nlon}
    )

    def send_plane(d, c):
        p = (me + d) % NP
        remote(meta, metas.at[me], ms, mr, plane(p)).start()
        return c

    def send_blocks(c):
        def one(d, carry):
            p = (me + d) % NP
            remote(pk.at[c, p], got.at[c, me], ss.at[c], sr.at[c], plane(p)).start()
            return carry

        lax.fori_loop(1, NP, one, 0)
        got[c, me] = pk[c, me]

    lax.fori_loop(1, NP, send_plane, 0)
    metas[me] = meta[...]
    send_blocks(0)
    @pl.when(top)
    def _():
        for a in range(4):

            @pl.when(there[a] != lon)
            def _():
                first_hop[a].start()

            @pl.when(there[a] == lon)
            def _():
                folda[a] = fold[...]

    send_blocks(1)
    send_blocks(2)
    to_south = remote(hsend.at[0], hgot.at[0], hs.at[0], hr.at[0], {"lat": jnp.maximum(lat - 1, 0)})
    to_north = remote(hsend.at[1], hgot.at[1], hs.at[1], hr.at[1], {"lat": jnp.minimum(lat + 1, nlat - 1)})

    @pl.when(jnp.logical_not(bottom))
    def _():
        to_south.start()

    @pl.when(jnp.logical_not(top))
    def _():
        to_north.start()


    load_h.wait()
    block, shifted = hinge[0] // W, hinge[0] % W
    digit = (block + 1) // 4

    @pl.when(top)
    def _():
        at = iota((W, WX), 1)
        at = jnp.where(at < W + 64, at, at - WX)
        for i in range(3):
            wide = W if i < 2 else 128
            mirror[pl.ds(i * W, wide), :] = jnp.where(
                iota((wide, WX), 0) + i * W == W + shifted - at[0:wide], 1.0, 0.0
            ).astype(BF16)

        def clear(g, c):
            hgot[0, g] = jnp.zeros((8, W), F32)
            return c

        lax.fori_loop(0, nfk // 4, clear, 0)

    @pl.when(bottom)
    def _():
        def fill(g, c):
            hgot[1, g] = pltpu.roll(hsend[0, g], 1, 0)
            return c

        lax.fori_loop(0, nfk // 4, fill, 0)

    take(metas.at[pl.ds(0, NP - 1)], mr)
    find = jnp.where(iota((128, N), 0) == me * nz + iota((128, N), 1) % nz, 1.0, 0.0).astype(BF16)
    known = jnp.dot(metas[...].reshape(NP * 8, 128).astype(BF16), find, preferred_element_type=F32)
    mine = iota((NP * 8, N), 1) // nz == (iota((NP * 8, N), 0) // 8) * 2 + iota((NP * 8, N), 0) % 8
    mine = mine & (iota((NP * 8, N), 0) % 8 < 2)
    named = jnp.sum(jnp.where(mine, known, 0.0), axis=0, keepdims=True)
    r_id = iota((nz * ROWS, N), 0)
    land = (r_id // ROWS == iota((nz * ROWS, N), 1) % nz) & ((r_id % ROWS + 1).astype(F32) == named)
    land = jnp.where(land, 1.0, 0.0).astype(BF16)
    land3 = jnp.concatenate([land, land, land], axis=1)

    ahead = nz // 2
    behind = nz - 1 - ahead

    def hop(c, s, up):
        out, into, send, recv, to = (
            (east_out, east_in, zes, zer, up_z) if up else (west_out, west_in, zws, zwr, down_z)
        )
        return remote(out.at[c, s], into.at[c, s], send.at[c, s], recv.at[c, s], to)

    def ring(c, s):
        for up, steps in ((True, ahead), (False, behind)):
            if s >= steps:
                continue
            out, into = (east_out, east_in) if up else (west_out, west_in)
            block = dense[c, (z + (steps - s if up else nz - steps + s)) % nz]
            if s > 0:
                hop(c, s - 1, up).wait_recv()
                block += into[c, s - 1]
            out[c, s] = block
            hop(c, s, up).start()

    def landed(c):
        take(got.at[c, pl.ds(0, NP - 1)], sr.at[c])
        hi, mid, low = split3(got[c].reshape(N, HW))
        out = jnp.dot(land3, jnp.concatenate([hi, mid, low], axis=0), preferred_element_type=F32)
        dense[c] = out.reshape(nz, ROWS, HW)

        ring(c, 0)

    for c in range(3):
        landed(c)

    @pl.when(top)
    def _():
        for a in range(4):

            @pl.when(there[a] != lon)
            def _():
                first_hop[a].wait_recv()

        def pick(g, c):
            foldm[g] = folda[digit % 4, g]
            foldb[2, g] = folda[digit % 4, g]
            return c

        lax.fori_loop(0, nfk // 4, pick, 0)
        for a in second_hop:
            a.start()
        third_hop.start()

    @pl.when(jnp.logical_not(top))
    def _():
        to_south.wait_recv()

    @pl.when(jnp.logical_not(bottom))
    def _():
        to_north.wait_recv()

    upper = iota((8, W), 0) < 4

    def rows_in(g, c):
        n, s = hgot[0, g], hgot[1, g]
        for i in range(4):
            X[4 * g + i, pl.ds(ROWS, 8), pl.ds(0, W)] = jnp.where(
                upper, pltpu.roll(n, (8 - 2 * i) % 8, 0), pltpu.roll(s, (6 - 2 * i) % 8, 0)
            )
        return c

    lax.fori_loop(0, nfk // 4, rows_in, 0)
    lane = iota((EXT, 128), 1)

    def cols_out(f, c):
        w, e = c
        for k in range(nk):
            at = f * (2 * nk) + 2 * k
            a = X[f * nk + k, :, pl.ds(0, 128)]
            b = X[f * nk + k, :, pl.ds(W - 128, 128)]
            here = lane // 2 == f * nk + k
            w = jnp.where(here, pltpu.roll(a, at, 1), w)
            e = jnp.where(here, pltpu.roll(b, (at + 2) % 128, 1), e)
        return w, e

    w, e = lax.fori_loop(0, 6, cols_out, (jnp.zeros((EXT, 128), F32), jnp.zeros((EXT, 128), F32)))
    esend[0] = w
    esend[1] = e
    to_west = remote(esend.at[0], egot.at[0], es.at[0], er.at[0], {"lon": (lon + nlon - 1) % nlon})
    to_east = remote(esend.at[1], egot.at[1], es.at[1], er.at[1], {"lon": (lon + 1) % nlon})
    to_west.start()
    to_east.start()

    for c in range(3):
        ring(c, 1)

    to_west.wait_recv()
    to_east.wait_recv()
    fe, fw = egot[0], egot[1]

    def cols_in(f, c):
        for k in range(nk):
            at = f * (2 * nk) + 2 * k
            X[f * nk + k, :, pl.ds(W, 128)] = jnp.where(
                lane < 64, pltpu.roll(fe, (128 - at) % 128, 1), pltpu.roll(fw, (254 - at) % 128, 1)
            )
        return c

    lax.fori_loop(0, 6, cols_in, 0)

    to_lower = remote(levs, levg, ls, lr, {"lev": 1})
    to_lower2 = remote(lev2s, lev2g, ps, pr, {"lev": 1})

    def shallower():
        levs[...] = ALPHA * X[2 * nk] - BETA * X[3 * nk]

        def add(k, c):
            levs[...] += ALPHA * X[2 * nk + k] - BETA * X[3 * nk + k]
            return c

        lax.fori_loop(1, nk, add, 0)
        to_lower.start()
        levg[...] = jnp.zeros((EXT, WX), F32)

    pl.when((lev == 0) & jnp.logical_not(top))(shallower)

    for s in range(2, ahead):
        for c in range(3):
            ring(c, s)

    for c in range(3):
        hop(c, ahead - 1, True).wait_recv()
        total = dense[c, z] + east_in[c, ahead - 1]
        if behind:
            hop(c, behind - 1, False).wait_recv()
            total += west_in[c, behind - 1]
        half[c] = total
    for i, r in enumerate((0, ROWS - 1)):
        frow[i] = jnp.concatenate(
            [half[c, pl.ds(r, 1), pl.ds(q * 128, 128)] for c in range(3) for q in range(2)]
            + [jnp.zeros((2, 128), F32)],
            axis=0,
        )
    to_partner = remote(half, partner, ps2(rs, 0), ps2(rr, 0), {"lev": other})
    to_partner.start()
    south_at = jnp.maximum(lat - 1, 0)
    north_at = jnp.minimum(lat + 1, nlat - 1)
    down = [remote(frow.at[0], rowsgot.at[0, lev], rs.at[1 + i], rr.at[1 + i], {"lat": south_at, "lev": lev if i == 0 else other}) for i in range(2)]
    up = [remote(frow.at[1], rowsgot.at[1, lev], rs.at[3 + i], rr.at[3 + i], {"lat": north_at, "lev": lev if i == 0 else other}) for i in range(2)]

    @pl.when(jnp.logical_not(bottom))
    def _():
        for a in down:
            a.start()

    @pl.when(jnp.logical_not(top))
    def _():
        for a in up:
            a.start()

    edge = half.at[:, :, pl.ds(pl.multiple_of(lev * (HW - 128), 128), 128)]
    edge_to = (lon + nlon - 1 + 2 * lev) % nlon
    sides = [remote(edge, colsgot.at[lev], cs.at[i], cr.at[lev], {"lon": edge_to, "lev": lev if i == 0 else other}) for i in range(2)]
    for a in sides:
        a.start()

    @pl.when(top)
    def _():
        def one(d, c):
            for i in range(2):
                remote(
                    frow.at[1], foldgot.at[lev, lon], fs, fr.at[i],
                    {"lon": (lon + d) % nlon, "lev": lev if i == 0 else other},
                ).start()
            return c

        lax.fori_loop(1, nlon, one, 0)
        foldgot[lev, lon] = frow[1]

    @pl.when(top)
    def _():
        for a in second_hop:
            a.wait_recv()
        third_hop.wait_recv()
        near = block - 4 * digit + 1
        out = jnp.zeros((2 * nfk, WX), F32)
        for i in range(3):
            wide = W if i < 2 else 128
            for part in split3(foldb[near + i, :, :, pl.ds(0, wide)].reshape(2 * nfk, wide)):
                out += jnp.dot(part, mirror[pl.ds(i * W, wide), :], preferred_element_type=F32)
        fold_rows[...] = out.reshape(nfk // 4, 8, WX)
        two = iota((8, WX), 0) < 2

        def insert(g, c):
            n = fold_rows[g]
            for i in range(4):
                X[4 * g + i, pl.ds(ROWS, 8), :] = jnp.where(
                    two, pltpu.roll(n, (8 - 2 * i) % 8, 0), X[4 * g + i, pl.ds(ROWS, 8), :]
                )
            return c

        lax.fori_loop(0, nfk // 4, insert, 0)

    pl.when((lev == 0) & top)(shallower)

    row_id = iota((EXT, WX), 0)
    turning = jnp.where(row_id == ROWS, X[5 * nk, pl.ds(17, 1), :], X[5 * nk, pl.ds(22, 1), :])
    for i in range(ROWS):
        turning = jnp.where(row_id == i, cor[i], turning)
    cors[...] = turning

    @pl.when(lev == 1)
    def _():
        to_lower.wait_recv()

    lev2s[...] = jnp.zeros((2, EXT, WX), F32)
    run = tail.at[0]
    run[...] = jnp.zeros((EXT, WX), F32)
    copy_row = (row_id == EXT - 1) & bottom

    def level(k, c):
        q = [X[f * nk + k] for f in range(5)]
        m = X[5 * nk + k]
        new, running = substep(q, m, levg[...], run[...], cors[...])
        run[...] = running
        new = [jnp.where(copy_row, a[0:1, :], a) for a in new]
        for f in range(5):
            X[f * nk + k] = new[f]
        lev2s[0] += ALPHA * new[2] - BETA * new[3]
        lev2s[1] += m * pen[k]
        return c

    lax.fori_loop(0, nk, level, 0)

    @pl.when(lev == 0)
    def _():
        to_lower2.start()
        lev2g[...] = jnp.zeros((2, EXT, WX), F32)

    FX[:, pl.ds(0, ROWS), pl.ds(pl.multiple_of(lev * HW, HW), HW)] = half[...]
    to_partner.wait_recv()
    FX[:, pl.ds(0, ROWS), pl.ds(pl.multiple_of(other * HW, HW), HW)] = partner[...]
    for i in range(2):
        pltpu.make_async_copy(colsgot.at[i], colsgot.at[i], cr.at[i]).wait()
    side = lax.broadcasted_iota(I32, (3, ROWS, 128), 2)
    FX[:, pl.ds(0, ROWS), pl.ds(W, 128)] = jnp.where(side < 64, colsgot[0], colsgot[1])

    first, last = iota((8, W), 0) == 0, iota((8, W), 0) == 7

    @pl.when(jnp.logical_not(bottom))
    def _():
        for i in range(2):
            up[i].wait_recv()

    @pl.when(jnp.logical_not(top))
    def _():
        for i in range(2):
            down[i].wait_recv()

    def joined(ref, c):
        return jnp.concatenate(
            [ref[h, pl.ds(2 * c + q, 1), pl.ds(0, 128)] for h in range(2) for q in range(2)], axis=1
        )

    @pl.when(top)
    def _():
        foldgot[other, lon] = jnp.concatenate(
            [partner[c, pl.ds(ROWS - 1, 1), pl.ds(q * 128, 128)] for c in range(3) for q in range(2)]
            + [jnp.zeros((2, 128), F32)],
            axis=0,
        )
        for i in range(2):
            take(foldgot.at[0, pl.ds(0, nlon - 1)], fr.at[i])
        b1 = (block + nlon - lon) % nlon
        b0 = (b1 + nlon - 1) % nlon
        outs = [jnp.zeros((24, W), F32), jnp.zeros((24, W), F32)]
        for i, b in enumerate((b0, b1)):
            for h in range(2):
                tile = jnp.concatenate(split3(foldgot[h, b]), axis=0)
                for q in range(2):
                    at = i * W + h * HW + q * 128
                    keep = jnp.where(iota((24, 128), 0) % 2 == q, tile.astype(F32), 0.0).astype(BF16)
                    outs[q] += jnp.dot(keep, mirror[pl.ds(at, 128), pl.ds(0, W)], preferred_element_type=F32)
        sums = [o[0:8] + o[8:16] + o[16:24] for o in outs]
        for c in range(3):
            rowsgot2(FX, c, sums[0][2 * c : 2 * c + 1] + sums[1][2 * c + 1 : 2 * c + 2], first, W)

    @pl.when(jnp.logical_not(top))
    def _():
        for c in range(3):
            rowsgot2(FX, c, joined(rowsgot.at[0], c), first, W)

    @pl.when(bottom)
    def _():
        for c in range(3):
            FX[c, pl.ds(ROWS, 8), pl.ds(0, W)] = jnp.where(
                last, FX[c, pl.ds(0, 1), pl.ds(0, W)], FX[c, pl.ds(ROWS, 8), pl.ds(0, W)]
            )

    @pl.when(jnp.logical_not(bottom))
    def _():
        for c in range(3):
            FX[c, pl.ds(ROWS, 8), pl.ds(0, W)] = jnp.where(
                last, joined(rowsgot.at[1], c), FX[c, pl.ds(ROWS, 8), pl.ds(0, W)]
            )

    FX[:, pl.ds(ROWS, 8), pl.ds(W, 128)] = jnp.zeros((3, 8, 128), F32)

    @pl.when(lev == 1)
    def _():
        to_lower2.wait_recv()

    extra = ALPHA * FX[0] - BETA * FX[1]
    tail[1] = lev2g[0] + lev2g[1] * extra
    tail[0] = jnp.zeros((EXT, WX), F32)

    def store(k):
        return pltpu.make_async_copy(outs.at[k % 2], result.at[:, k], ds.at[k % 2])

    def finish(k, c):
        m = X[5 * nk + k]
        gain = m * pen[k]
        push = [gain * FX[i] for i in range(3)]
        q = [X[f * nk + k] + push[f - 2] if f > 1 else X[f * nk + k] for f in range(5)]
        new, running = substep(q, m, tail[1], tail[0], cors[...])
        tail[0] = running

        @pl.when(k >= 2)
        def _():
            store(k - 2).wait()

        for f in range(5):
            value = new[f] + push[f - 2] if f > 1 else new[f]
            outs[k % 2, f] = value[0:ROWS, 0:W]
        store(k).start()
        return c

    lax.fori_loop(0, nk, finish, 0)

    store(nk - 2).wait()
    store(nk - 1).wait()

    take(metas.at[pl.ds(0, NP - 1)], ms)
    for c in range(3):
        take(pk.at[c, pl.ds(0, NP - 1)], ss.at[c])
    for c in range(3):
        for s in range(ahead):
            hop(c, s, True).wait_send()
        for s in range(behind):
            hop(c, s, False).wait_send()
    to_west.wait_send()
    to_east.wait_send()
    to_partner.wait_send()
    for a in sides:
        a.wait_send()

    @pl.when(lev == 0)
    def _():
        to_lower.wait_send()
        to_lower2.wait_send()

    @pl.when(jnp.logical_not(bottom))
    def _():
        to_south.wait_send()
        for a in down:
            a.wait_send()

    @pl.when(jnp.logical_not(top))
    def _():
        to_north.wait_send()
        for a in up:
            a.wait_send()

    @pl.when(top)
    def _():
        take(foldgot.at[:, pl.ds(0, nlon - 1)], fs)
        for a in range(4):

            @pl.when(there[a] != lon)
            def _():
                first_hop[a].wait_send()

        for a in second_hop:
            a.wait_send()
        third_hop.wait_send()


def ps2(ref, i):
    return ref.at[i]


def rowsgot2(FX, c, line, first, W):
    FX[c, pl.ds(ROWS, 8), pl.ds(0, W)] = jnp.where(first, line, 0.0)


def body(state, mask, coriolis, penetration, flux_tiles, flux_owner, flux_row, fold_partner):
    _, nk, rows, W = state.shape
    nlon, nlat = lax.axis_size("lon"), lax.axis_size("lat")
    tiles = flux_tiles.shape[0]
    nz, NP = nlon // 2, 2 * nlat
    N, HW, WX, nfk = NP * 2 * nz, W // 2, W + 128, 6 * nk

    up, down = nz // 2, max(1, nz - 1 - nz // 2)
    hbm = pl.BlockSpec(memory_space=pl.ANY)
    V = lambda *s: pltpu.VMEM(s, F32)
    D = lambda *s: pltpu.SemaphoreType.DMA(s)
    return pl.pallas_call(
        functools.partial(exchange_kernel, nlon, nlat, tiles, nk, W),
        out_shape=jax.ShapeDtypeStruct(state.shape, F32),
        in_specs=[hbm] * 8,
        out_specs=hbm,
        scratch_shapes=[
            V(nfk, EXT, WX), V(3, EXT, WX), V(2, EXT, WX), V(2, 5, ROWS, W),
            V(3, tiles, HW), pltpu.VMEM((nk, ROWS, W), I32),
            V(3, NP, 2 * nz, HW), V(3, NP, 2 * nz, HW), V(8, 128), V(NP, 8, 128),
            V(3, nz, ROWS, HW), V(3, up, ROWS, HW), V(3, up, ROWS, HW), V(3, down, ROWS, HW), V(3, down, ROWS, HW),
            V(3, ROWS, HW), V(3, ROWS, HW),
            V(2, 8, 128), V(2, 2, 8, 128), V(2, 3, ROWS, 128), V(2, nlon, 8, 128),
            V(2, nfk // 4, 8, W), V(2, nfk // 4, 8, W),
            V(nfk // 4, 8, W), V(4, nfk // 4, 8, W), V(nfk // 4, 8, W), V(6, nfk // 4, 8, W), V(nfk // 4, 8, WX), pltpu.SMEM((1024,), I32),
            pltpu.SMEM((ROWS,), F32), pltpu.SMEM((nk,), F32), pltpu.VMEM((1, tiles), I32), pltpu.VMEM((1, tiles), I32),
            V(2, EXT, 128), V(2, EXT, 128),
            V(EXT, WX), V(EXT, WX), V(2, EXT, WX), V(2, EXT, WX), V(EXT, WX), pltpu.VMEM((2 * W + 128, WX), BF16),
            D(8), pltpu.SemaphoreType.DMA, pltpu.SemaphoreType.DMA, D(3), D(3), D(3, up), D(3, up), D(3, down), D(3, down), D(2), D(2), D(2), D(2),
            pltpu.SemaphoreType.DMA, pltpu.SemaphoreType.DMA, pltpu.SemaphoreType.DMA, pltpu.SemaphoreType.DMA,
            D(5), D(5), D(2), D(2), pltpu.SemaphoreType.DMA, D(2), D(4), D(4), D(5), D(5), D(2),
        ],
        compiler_params=pltpu.CompilerParams(
            collective_id=0, has_side_effects=True, vmem_limit_bytes=60 * 1024 * 1024
        ),
        name="exchange",
    )(
        state.reshape(5 * nk, rows, W), mask, coriolis, penetration, flux_tiles.transpose(1, 0, 2),
        flux_owner.reshape(1, tiles), flux_row.reshape(1, tiles), fold_partner,
    )


def solution(mesh):
    return jax.shard_map(
        body,
        mesh=mesh,
        in_specs=(
            P(None, "lev", "lat", "lon"),
            P("lev", "lat", "lon"),
            P("lat"),
            P("lev"),
            P(("lon", "lat"), None, None),
            P(("lon", "lat"), None),
            P(("lon", "lat")),
            P(),
        ),
        out_specs=P(None, "lev", "lat", "lon"),
        check_vma=False,
    )
```
